512 devices in a mesh: side: 2 (over x_hi), row: 16 (over z), col: 16 (over x_lo, y, core).
Axes of the slice: x: 4 (x_hi: 2, x_lo: 2; x = x_hi * 2 + x_lo), y: 4, z: 16, core: 2. Of those that a mesh axis runs over, the one named last changes fastest.
Arguments:
- query: bfloat16 [2, 32, 4096], P(None, 'row'), may hold values from -32 to 32
- new_keys: bfloat16 [2, 32, 512], P(None, 'row'), may hold values from -6 to 6
- new_values: bfloat16 [2, 32, 512], P(None, 'row'), may hold values from -12 to 12
- key_cache: bfloat16 [32, 6144, 512], P('row', 'col'), may hold values from -4 to 4
- value_cache: bfloat16 [32, 6144, 512], P('row', 'col'), may hold values from -12 to 12
- lengths: int32 [32], P('row'), may hold values from 1024 to 6144, as said below
- residual: bfloat16 [2, 32, 8192], P(None, None, 'row'), may hold values from -32 to 32
- out_weight: bfloat16 [4096, 8192], P('col', 'row'), may hold values from -0.5 to 0.5
- norm_gain: bfloat16 [8192], P('row'), may hold values from 0.099609375 to 1.8984375
- gate_weight: bfloat16 [8192, 14336], P('row', 'col'), may hold values from -0.0625 to 0.0625
- up_weight: bfloat16 [8192, 14336], P('row', 'col'), may hold values from -0.0625 to 0.0625
- down_weight: bfloat16 [14336, 8192], P('col', 'row'), may hold values from -0.046875 to 0.046875
Outputs:
- hidden_out: bfloat16 [2, 32, 8192], P(None, None, 'row')
The draws below stay inside these ranges and needn't reach their ends.
Inputs may be any that keep to these rules, and one draw needn't show every extreme that they name: `lengths`: every value from 1024 to 6144 can occur; in every draw some row has exactly 6144 and some row exactly 1024.
All inputs are finite; a program needn't handle non-finite values.
Results may differ from the reference program's by a relative error of at most 0.0059.
Values may be sent and summed in bfloat16 or wider, within the bound.
A program may use at most 64 MiB of HBM per device.

```python
import math
import jax
import jax.numpy as jnp
from jax import lax

D = 8192
FF = 14336
HEADS = 32
KV_HEADS = 4
HD = 128
ROWS = 32
CAP = 6144
MINLEN = 1024


def draw_lengths(key, part):
    key = jax.random.fold_in(key, 5)
    first, second = jax.random.split(key)
    drawn = jax.random.randint(first, (ROWS,), MINLEN, CAP + 1)
    order = jax.random.permutation(second, ROWS)
    drawn = drawn.at[order[0]].set(CAP)
    drawn = drawn.at[order[1]].set(MINLEN)
    return drawn.astype(jnp.int32)


def draw_key_cache(key, part):
    own = jax.random.fold_in(key, 11)
    base = jax.random.truncated_normal(own, -4.0, 4.0, (ROWS, CAP, KV_HEADS * HD), jnp.float32)
    return base.astype(jnp.bfloat16)


def draw_query(key, part):
    own = jax.random.fold_in(key, 12)
    base = jax.random.truncated_normal(own, -4.0, 4.0, (2, ROWS, HEADS * HD), jnp.float32)
    return base.astype(jnp.bfloat16)


def draw_residual(key, part):
    key = jax.random.fold_in(key, 7)
    first, second, third = jax.random.split(key, 3)
    ramp = jnp.arange(D, dtype=jnp.float32) / D
    rough = jnp.exp(jax.random.uniform(second, (D,), jnp.float32, -0.35, 0.35))
    values = jax.random.truncated_normal(first, -4.0, 4.0, (2, ROWS, D), jnp.float32)
    columns = 0.5 * jnp.exp(ramp * math.log(3.0)) * rough
    rows = 0.3 * jnp.exp(jax.random.uniform(third, (2, ROWS), jnp.float32, 0.0, math.log(10.0)))
    return (values * rows[:, :, None] * columns[None, None, :]).astype(jnp.bfloat16)


def shard_levels(stream_key, extent, cuts, least, high):
    gain = 1.0
    for axis_at, parts in cuts:
        heights = jax.random.uniform(jax.random.fold_in(jax.random.fold_in(stream_key, 6), axis_at), (parts,), jnp.float32, least / len(cuts), high / len(cuts))
        gain = gain * jnp.repeat(jnp.exp(heights), extent[axis_at] // parts).reshape((-1,) + (1,) * (len(extent) - 1 - axis_at))
    return gain


def gaussian(own_key, extent, width, limit, cuts=(), kind=jnp.bfloat16):
    array = width * jax.random.normal(own_key, extent, jnp.float32)
    if cuts:
        array = array * shard_levels(own_key, extent, cuts, -0.22, 0.18)
    return jnp.clip(array, -limit, limit).astype(kind)


def setup_inputs(seed: int = 0) -> dict:
    key_list = jax.random.split(jax.random.key(seed), 13)
    query = draw_query(jax.random.fold_in(key_list[12], 71), 0)
    new_keys = gaussian(key_list[1], (2, ROWS, KV_HEADS * HD), 1.0, 6.0, ((1, 16),))
    new_values = gaussian(key_list[2], (2, ROWS, KV_HEADS * HD), 2.0, 12.0, ((1, 16),))
    key_cache = draw_key_cache(jax.random.fold_in(key_list[12], 71), 0)
    value_cache = gaussian(key_list[4], (ROWS, CAP, KV_HEADS * HD), 2.0, 12.0, ((0, 16), (1, 16)))
    lengths = draw_lengths(jax.random.fold_in(key_list[12], 71), 0)
    residual = draw_residual(jax.random.fold_in(key_list[12], 71), 0)
    out_weight = gaussian(key_list[7], (HEADS * HD, D), HD ** -0.5, 0.5, ((0, 16), (1, 16)))
    norm_gain = jnp.clip(1.0 + 0.18 * jax.random.normal(key_list[8], (D,), jnp.float32), 0.099609375, 1.8984375).astype(jnp.bfloat16)
    gate_weight = gaussian(key_list[9], (D, FF), D ** -0.5, 0.0625, ((0, 16), (1, 16)))
    up_weight = gaussian(key_list[10], (D, FF), D ** -0.5, 0.0625, ((0, 16), (1, 16)))
    down_weight = gaussian(key_list[11], (FF, D), FF ** -0.5, 0.046875, ((0, 16), (1, 16)))
    return {"query": query, "new_keys": new_keys, "new_values": new_values, "key_cache": key_cache, "value_cache": value_cache, "lengths": lengths, "residual": residual, "out_weight": out_weight, "norm_gain": norm_gain, "gate_weight": gate_weight, "up_weight": up_weight, "down_weight": down_weight}


def reference(query, new_keys, new_values, key_cache, value_cache, lengths, residual, out_weight, norm_gain, gate_weight, up_weight, down_weight):
    group = HEADS // KV_HEADS
    inv_root = 1.0 / math.sqrt(HD)
    positions = jnp.arange(CAP, dtype=jnp.int32)
    live = positions[None, :] < lengths.astype(jnp.int32)[:, None]
    cached_keys = key_cache.astype(jnp.float32).reshape(ROWS, CAP, KV_HEADS, HD)
    cached_values = value_cache.astype(jnp.float32).reshape(ROWS, CAP, KV_HEADS, HD)
    finished = []
    for step in range(2):
        queries = query[step].astype(jnp.float32).reshape(ROWS, KV_HEADS, group, HD)
        cache_scores = jnp.einsum('bkgd,bpkd->bkgp', queries, cached_keys, precision=lax.Precision.HIGHEST) * inv_root
        cache_scores = jnp.where(live[:, None, None, :], cache_scores, -jnp.inf)
        fresh_keys = new_keys[:step + 1].astype(jnp.float32).reshape(step + 1, ROWS, KV_HEADS, HD)
        fresh_values = new_values[:step + 1].astype(jnp.float32).reshape(step + 1, ROWS, KV_HEADS, HD)
        fresh_scores = jnp.einsum('bkgd,tbkd->bkgt', queries, fresh_keys, precision=lax.Precision.HIGHEST) * inv_root
        top = jnp.maximum(lax.optimization_barrier(jnp.max(cache_scores, axis=-1)), lax.optimization_barrier(jnp.max(fresh_scores, axis=-1)))
        cache_weights = jnp.exp(cache_scores - top[..., None])
        fresh_weights = jnp.exp(fresh_scores - top[..., None])
        total = lax.optimization_barrier(jnp.sum(cache_weights, axis=-1)) + lax.optimization_barrier(jnp.sum(fresh_weights, axis=-1))
        summed = jnp.einsum('bkgp,bpkd->bkgd', cache_weights, cached_values, precision=lax.Precision.HIGHEST)
        summed = summed + jnp.einsum('bkgt,tbkd->bkgd', fresh_weights, fresh_values, precision=lax.Precision.HIGHEST)
        attended = (summed / total[..., None]).reshape(ROWS, HEADS * HD).astype(jnp.bfloat16)
        mid = residual[step].astype(jnp.float32) + jnp.dot(attended, out_weight, preferred_element_type=jnp.float32)
        inv = lax.rsqrt(lax.optimization_barrier(jnp.mean(mid * mid, axis=1, keepdims=True)) + 1e-05)
        lifted = (mid * norm_gain.astype(jnp.float32)).astype(jnp.bfloat16)
        gate = jnp.dot(lifted, gate_weight, preferred_element_type=jnp.float32) * inv
        up = jnp.dot(lifted, up_weight, preferred_element_type=jnp.float32) * inv
        act = (jax.nn.silu(gate) * up).astype(jnp.bfloat16)
        finished.append((mid + jnp.dot(act, down_weight, preferred_element_type=jnp.float32)).astype(jnp.bfloat16))
    return jnp.stack(finished)
```

```python
import functools
import math

import jax
import jax.numpy as jnp
from jax import lax
from jax.experimental import pallas as pl
from jax.experimental.pallas import tpu as pltpu
from jax.sharding import PartitionSpec as P

D = 8192
KV = 4
HD = 128
N = 16
SPAN = 384
VERY_LOW = -1e30
F32 = jnp.float32
BF16 = jnp.bfloat16
MESH = pl.DeviceIdType.MESH


def kernel(
    len_ref, q_hbm, nk_hbm, nv_hbm, k_hbm, v_hbm, res_hbm, ow_hbm, gain_hbm, gw_hbm, uw_hbm, dw_hbm,
    out_ref,
    q_v, nk_v, nv_v, k_v, v_v, res_v, ow_v, gain_v, gw_v, uw_v, dw_v,
    qbd, heads, resp,
    st_a, rc_a, st_b, rc_b, st_c, rc_c, st_d, rc_d, st_e32, st_e, rc_e, st_f, rc_f, f32f, st_g, rc_g, st_h,
    load_sem, send_sem, recv_sem,
):
    s = lax.axis_index("side")
    r = lax.axis_index("row")
    c = lax.axis_index("col")

    loads = [
        pltpu.make_async_copy(src, dst, load_sem.at[i])
        for i, (src, dst) in enumerate(
            [
                (q_hbm, q_v),
                (k_hbm.at[s], k_v),
                (v_hbm.at[s], v_v),
                (nk_hbm, nk_v),
                (nv_hbm, nv_v),
                (res_hbm, res_v),
                (gain_hbm, gain_v),
                (ow_hbm, ow_v),
                (gw_hbm, gw_v),
                (uw_hbm, uw_v),
                (dw_hbm, dw_v),
            ]
        )
    ]
    for copy in loads:
        copy.start()

    barrier = pltpu.get_barrier_semaphore()

    def greet_row(i, _):
        pl.semaphore_signal(barrier, inc=1, device_id=(s, lax.rem(r + i, N), c), device_id_type=MESH)
        return 0

    def greet_col(i, _):
        other = lax.rem(s * N + c + i, 2 * N)
        pl.semaphore_signal(
            barrier, inc=1, device_id=(other // N, r, lax.rem(other, N)), device_id_type=MESH
        )
        return 0

    lax.fori_loop(1, N, greet_row, 0)
    lax.fori_loop(1, 2 * N, greet_col, 0)

    def exchange(phase, source, target, peer_id):
        def one(i, _):
            peer = peer_id(i)
            pltpu.make_async_remote_copy(
                src_ref=source(peer),
                dst_ref=target,
                send_sem=send_sem.at[phase],
                recv_sem=recv_sem.at[phase],
                device_id=(s, r, peer) if phase in COL_PHASES else (s, peer, c),
                device_id_type=MESH,
            ).start()
            return 0

        lax.fori_loop(1, N, one, 0)

    COL_PHASES = (0, 2, 3, 6)

    def col_peer(i):
        return lax.rem(c + i, N)

    def row_peer(i):
        return lax.rem(r + i, N)

    def rows_at(ref, at, rows):
        return ref.at[pl.ds(pl.multiple_of(at * rows, rows), rows)]

    def arrived(phase, ref):
        pltpu.make_async_copy(ref, ref, recv_sem.at[phase]).wait()

    qbd[...] = jnp.zeros_like(qbd)
    loads[0].wait()
    query = q_v[...].astype(F32)
    for t in range(2):
        mine = jnp.where(s == 0, query[t, 0:1, :], query[t, 1:2, :])
        for h in range(KV * 8):
            g = h // 8
            one_head = mine[:, h * HD : (h + 1) * HD]
            qbd[2 * h + t : 2 * h + t + 1, g * HD : (g + 1) * HD] = one_head
            heads[h // 2, 2 * (h % 2) + t : 2 * (h % 2) + t + 1, :] = one_head
    loads[1].wait()
    scale = 1.0 / math.sqrt(HD)
    scores = (
        lax.dot_general(
            qbd[...].astype(BF16), k_v[...], (((1,), (1,)), ((), ())), preferred_element_type=F32
        )
        * scale
    )
    live = c * SPAN + lax.broadcasted_iota(jnp.int32, scores.shape, 1) < len_ref[s]
    scores = jnp.where(live, scores, VERY_LOW)
    peak = jnp.max(scores, axis=1, keepdims=True)
    weights = jnp.where(live, jnp.exp(scores - peak), 0.0)
    total = jnp.sum(weights, axis=1, keepdims=True)
    loads[2].wait()
    summed = jnp.dot(weights.astype(BF16), v_v[...], preferred_element_type=F32)
    low_lane = lax.broadcasted_iota(jnp.int32, (64, HD), 1) < HD // 2
    stats = jnp.where(low_lane, peak, total)
    for o in range(N):
        g = o // 4
        st_a[8 * o : 8 * o + 4, :] = summed[4 * o : 4 * o + 4, g * HD : (g + 1) * HD]
        st_a[8 * o + 4 : 8 * o + 8, :] = stats[4 * o : 4 * o + 4, :]

    pl.semaphore_wait(barrier, 3 * N - 2)
    exchange(0, lambda peer: rows_at(st_a, peer, 8), rows_at(rc_a, c, 8), col_peer)
    rows_at(rc_a, c, 8)[...] = rows_at(st_a, c, 8)[...]

    group_lanes = pl.ds(pl.multiple_of((c // 4) * HD, HD), HD)
    for copy in loads[3:8]:
        copy.wait()
    q4 = heads[c]
    fresh_k = nk_v[:, :, group_lanes].astype(F32)
    fresh_v = nv_v[:, :, group_lanes].astype(F32)
    nk = [jnp.where(s == 0, fresh_k[t, 0:1, :], fresh_k[t, 1:2, :]) for t in range(2)]
    nv = [jnp.where(s == 0, fresh_v[t, 0:1, :], fresh_v[t, 1:2, :]) for t in range(2)]
    second = lax.rem(lax.broadcasted_iota(jnp.int32, (4, HD), 0), 2) == 1
    f0 = jnp.broadcast_to(jnp.sum(q4 * nk[0], axis=1, keepdims=True) * scale, (4, HD))
    f1 = jnp.broadcast_to(jnp.sum(q4 * nk[1], axis=1, keepdims=True) * scale, (4, HD))
    f1 = jnp.where(second, f1, VERY_LOW)
    own_row = lax.broadcasted_iota(jnp.int32, (2 * N, 512), 0) == 2 * c + s
    for t in range(2):
        row = jnp.sum(jnp.where(own_row, res_v[t].astype(F32), 0.0), axis=0, keepdims=True)
        for k in range(4):
            resp[2 * k + t : 2 * k + t + 1, :] = row[:, k * HD : (k + 1) * HD]
    gains = gain_v[...].astype(F32).reshape(1, 512)

    arrived(0, rc_a.at[pl.ds(0, 8 * (N - 1))])
    blocks = rc_a[...].reshape(N, 8, HD)
    sums, stat = blocks[:, 0:4, :], blocks[:, 4:8, :]
    low = lax.broadcasted_iota(jnp.int32, (N, 4, HD), 2) < HD // 2
    turned = pltpu.roll(stat, HD // 2, 2)
    peaks = jnp.where(low, stat, turned)
    totals = jnp.where(low, turned, stat)
    top = jnp.maximum(jnp.max(peaks, axis=0), jnp.maximum(f0, f1))
    share = jnp.exp(peaks - top[None])
    e0 = jnp.exp(f0 - top)
    e1 = jnp.where(second, jnp.exp(f1 - top), 0.0)
    whole = jnp.sum(share * totals, axis=0) + e0 + e1
    mixed = jnp.sum(share * sums, axis=0) + e0 * nv[0] + e1 * nv[1]
    st_b[...] = (mixed / whole).astype(BF16).astype(F32)

    exchange(1, lambda peer: st_b, rc_b.at[r], row_peer)
    rc_b[r] = st_b[...]
    arrived(1, rc_b.at[pl.ds(0, N - 1)])

    def gather(ref, count, stride):
        return jnp.concatenate(
            [
                jnp.concatenate(
                    [ref[pl.ds(2 * k + t, N, stride=stride), :] for k in range(count)], axis=1
                )
                for t in range(2)
            ],
            axis=0,
        )

    def scatter(ref, value, count, stride, base=0):
        for t in range(2):
            for k in range(count):
                ref[pl.ds(base + 2 * k + t, N, stride=stride), :] = value[
                    N * t : N * (t + 1), k * HD : (k + 1) * HD
                ]

    attended = jnp.concatenate(
        [jnp.concatenate([rc_b[:, 2 * j + t, :] for j in range(2)], axis=1) for t in range(2)], axis=0
    )
    part = jnp.dot(attended.astype(BF16), ow_v[...], preferred_element_type=F32)
    scatter(st_c, part, 4, 8)
    exchange(2, lambda peer: rows_at(st_c, peer, 8), rows_at(rc_c, c, 8), col_peer)
    rows_at(rc_c, c, 8)[...] = rows_at(st_c, c, 8)[...]
    arrived(2, rc_c.at[pl.ds(0, 8 * (N - 1))])
    mid_piece = resp[...] + jnp.sum(rc_c[...].reshape(N, 8, HD), axis=0)

    st_d[...] = mid_piece
    exchange(3, lambda peer: st_d, rows_at(rc_d, c, 8), col_peer)
    rows_at(rc_d, c, 8)[...] = st_d[...]
    arrived(3, rc_d.at[pl.ds(0, 8 * (N - 1))])
    mid = gather(rc_d, 4, 8)
    lifted = (mid * gains).astype(BF16)
    squares = jnp.broadcast_to(jnp.sum(mid * mid, axis=1, keepdims=True), (2 * N, HD))
    squares_high = squares.astype(BF16).astype(F32)
    scatter(st_e32, squares_high, 1, 32, 14)
    scatter(st_e32, squares - squares_high, 1, 32, 30)
    loads[8].wait()
    scatter(st_e32, jnp.dot(lifted, gw_v[...], preferred_element_type=F32), 7, 32)
    loads[9].wait()
    scatter(st_e32, jnp.dot(lifted, uw_v[...], preferred_element_type=F32), 7, 32, 16)
    st_e[...] = st_e32[...].astype(BF16)
    exchange(4, lambda peer: rows_at(st_e, peer, 32), rows_at(rc_e, r, 32), row_peer)
    rows_at(rc_e, r, 32)[...] = rows_at(st_e, r, 32)[...]
    arrived(4, rc_e.at[pl.ds(0, 32 * (N - 1))])
    lifts = jnp.sum(rc_e[...].astype(F32).reshape(N, 32, HD), axis=0)
    gate, up = lifts[0:16], lifts[16:32]
    inv0 = lax.rsqrt((gate[14:15] + up[14:15]) / D + 1e-05)
    inv1 = lax.rsqrt((gate[15:16] + up[15:16]) / D + 1e-05)
    odd = lax.rem(lax.broadcasted_iota(jnp.int32, (16, HD), 0), 2) == 1
    inv = jnp.where(odd, inv1, inv0)
    gate, up = gate * inv, up * inv
    st_f[...] = (gate / (1.0 + jnp.exp(-gate)) * up).astype(BF16)

    exchange(5, lambda peer: st_f, rows_at(rc_f, r, 16), row_peer)
    rows_at(rc_f, r, 16)[...] = st_f[...]
    loads[10].wait()
    arrived(5, rc_f.at[pl.ds(0, 16 * (N - 1))])
    f32f[...] = rc_f[...].astype(F32)
    act = gather(f32f, 7, 16).astype(BF16)
    scatter(st_g, jnp.dot(act, dw_v[...], preferred_element_type=F32), 4, 8)
    exchange(6, lambda peer: rows_at(st_g, peer, 8), rows_at(rc_g, c, 8), col_peer)
    rows_at(rc_g, c, 8)[...] = rows_at(st_g, c, 8)[...]
    arrived(6, rc_g.at[pl.ds(0, 8 * (N - 1))])
    st_h[...] = (st_d[...] + jnp.sum(rc_g[...].reshape(N, 8, HD), axis=0)).astype(BF16)

    here = s * N + c

    def give(i, _):
        other = lax.rem(here + i, 2 * N)
        pltpu.make_async_remote_copy(
            src_ref=st_h,
            dst_ref=out_ref.at[here],
            send_sem=send_sem.at[7],
            recv_sem=recv_sem.at[7],
            device_id=(other // N, r, lax.rem(other, N)),
            device_id_type=MESH,
        ).start()
        return 0

    lax.fori_loop(1, 2 * N, give, 0)
    out_ref[here] = st_h[...]

    def sent(phase, ref):
        pltpu.make_async_copy(ref, ref, send_sem.at[phase]).wait()

    sent(0, rc_a.at[pl.ds(0, 8 * (N - 1))])
    sent(1, rc_b.at[pl.ds(0, N - 1)])
    sent(2, rc_c.at[pl.ds(0, 8 * (N - 1))])
    sent(3, rc_d.at[pl.ds(0, 8 * (N - 1))])
    sent(4, rc_e.at[pl.ds(0, 32 * (N - 1))])
    sent(5, rc_f.at[pl.ds(0, 16 * (N - 1))])
    sent(6, rc_g.at[pl.ds(0, 8 * (N - 1))])
    arrived(7, out_ref.at[pl.ds(0, 2 * N - 1)])
    sent(7, out_ref.at[pl.ds(0, 2 * N - 1)])


def shards(query, new_keys, new_values, key_cache, value_cache, lengths, residual, out_weight,
           norm_gain, gate_weight, up_weight, down_weight):
    def vm(*shape, kind=F32):
        return pltpu.VMEM(shape, kind)

    hbm = pl.BlockSpec(memory_space=pl.ANY)
    pieces = pl.pallas_call(
        kernel,
        out_shape=jax.ShapeDtypeStruct((2 * N, 8, HD), BF16),
        in_specs=[pl.BlockSpec(memory_space=pltpu.SMEM)] + [hbm] * 11,
        out_specs=pl.BlockSpec(memory_space=pltpu.VMEM),
        scratch_shapes=[
            vm(2, 2, 4096, kind=BF16),
            vm(2, 2, 512, kind=BF16),
            vm(2, 2, 512, kind=BF16),
            vm(SPAN, 512, kind=BF16),
            vm(SPAN, 512, kind=BF16),
            vm(2, 32, 512, kind=BF16),
            vm(256, 512, kind=BF16),
            vm(512, kind=BF16),
            vm(512, 896, kind=BF16),
            vm(512, 896, kind=BF16),
            vm(896, 512, kind=BF16),
            vm(64, 512),
            vm(N, 4, HD),
            vm(8, HD),
            vm(8 * N, HD), vm(8 * N, HD),
            vm(4, HD), vm(N, 4, HD),
            vm(8 * N, HD), vm(8 * N, HD),
            vm(8, HD), vm(8 * N, HD),
            vm(32 * N, HD), vm(32 * N, HD, kind=BF16), vm(32 * N, HD, kind=BF16),
            vm(16, HD, kind=BF16), vm(16 * N, HD, kind=BF16), vm(16 * N, HD),
            vm(8 * N, HD), vm(8 * N, HD),
            vm(8, HD, kind=BF16),
            pltpu.SemaphoreType.DMA((11,)),
            pltpu.SemaphoreType.DMA((8,)),
            pltpu.SemaphoreType.DMA((8,)),
        ],
        compiler_params=pltpu.CompilerParams(
            collective_id=0, has_side_effects=True, vmem_limit_bytes=40 * 1024 * 1024
        ),
        name="layer",
    )(lengths, query, new_keys, new_values, key_cache, value_cache, residual, out_weight, norm_gain,
      gate_weight, up_weight, down_weight)
    pieces = pieces.reshape(2, N, 4, 2, HD)
    return pieces.transpose(3, 1, 0, 2, 4).reshape(2, 2 * N, 512)


def solution(mesh):
    in_specs = (
        P(None, "row", None),
        P(None, "row", None),
        P(None, "row", None),
        P("row", "col", None),
        P("row", "col", None),
        P("row"),
        P(None, None, "row"),
        P("col", "row"),
        P("row"),
        P("row", "col"),
        P("row", "col"),
        P("col", "row"),
    )
    out_specs = P(None, None, "row")
    return jax.shard_map(shards, mesh=mesh, in_specs=in_specs, out_specs=out_specs, check_vma=False)
```

```python
import functools
import math

import jax
import jax.numpy as jnp
from jax import lax
from jax.experimental import pallas as pl
from jax.experimental.pallas import tpu as pltpu
from jax.sharding import PartitionSpec as P

D = 8192
KV = 4
HD = 128
N = 16
SPAN = 384
VERY_LOW = -1e30
F32 = jnp.float32
BF16 = jnp.bfloat16
MESH = pl.DeviceIdType.MESH


def kernel(
    len_hbm, q_hbm, nk_hbm, nv_hbm, k_hbm, v_hbm, res_hbm, ow_hbm, gain_hbm, gw_hbm, uw_hbm, dw_hbm,
    out_ref,
    len_ref, q_v, nk_v, nv_v, k_v, v_v, res_v, ow_v, gain_v, gw_v, uw_v, dw_v,
    qbd, heads, resp,
    st_a, rc_a, st_b, rc_b, st_c, rc_c, st_d, rc_d, st_e32, st_e, rc_e, st_f, rc_f, f32f, st_g, rc_g, st_h,
    load_sem, send_sem, recv_sem, met_sem,
):
    s = lax.axis_index("side")
    r = lax.axis_index("row")
    c = lax.axis_index("col")

    loads = [
        pltpu.make_async_copy(src, dst, load_sem.at[i])
        for i, (src, dst) in enumerate(
            [
                (q_hbm, q_v),
                (k_hbm.at[s], k_v),
                (v_hbm.at[s], v_v),
                (nk_hbm, nk_v),
                (nv_hbm, nv_v),
                (res_hbm, res_v),
                (gain_hbm, gain_v),
                (ow_hbm, ow_v),
                (gw_hbm, gw_v),
                (uw_hbm, uw_v),
                (dw_hbm, dw_v),
                (len_hbm, len_ref),
            ]
        )
    ]
    for copy in loads:
        copy.start()

    barrier = pltpu.get_barrier_semaphore()

    odd = lax.rem(c, 2)

    def greet_row(i, _):
        pl.semaphore_signal(
            barrier, inc=1, device_id=(s, lax.rem(r + i, N), c - odd + 1), device_id_type=MESH
        )
        return 0

    def greet_col(i, _):
        other = lax.rem(s * N + c + odd + i, 2 * N)
        pl.semaphore_signal(
            barrier, inc=1, device_id=(other // N, r, lax.rem(other, N)), device_id_type=MESH
        )
        return 0

    lax.fori_loop(1, N, lambda i, _: greet_col(2 * i, 0), 0)

    @pl.when(odd == 1)
    def _():
        greet_col(0, 0)

    @pl.when(odd == 0)
    def _():
        pl.semaphore_signal(barrier, inc=1, device_id=(s, r, c + 1), device_id_type=MESH)

    lax.fori_loop(1, N, greet_row, 0)

    def met_columns():
        @pl.when(odd == 0)
        def _():
            pl.semaphore_wait(barrier, 2 * N - 1)
            pl.semaphore_signal(met_sem, inc=1, device_id=(s, r, c + 1), device_id_type=MESH)

        @pl.when(odd == 1)
        def _():
            pl.semaphore_wait(met_sem, 1)

    def met_rows():
        @pl.when(odd == 1)
        def _():
            pl.semaphore_wait(barrier, 2 * N - 1)
            pl.semaphore_signal(met_sem, inc=1, device_id=(s, r, c - 1), device_id_type=MESH)

        @pl.when(odd == 0)
        def _():
            pl.semaphore_wait(met_sem, 1)

    def exchange(phase, source, target, peer_id):
        def one(i, _):
            half = (i + 1) // 2
            peer = peer_id(N // 2 + half * (1 - 2 * lax.rem(i, 2)))
            pltpu.make_async_remote_copy(
                src_ref=source(peer),
                dst_ref=target,
                send_sem=send_sem.at[phase],
                recv_sem=recv_sem.at[phase],
                device_id=(s, r, peer) if phase in COL_PHASES else (s, peer, c),
                device_id_type=MESH,
            ).start()
            return 0

        lax.fori_loop(0, N - 1, one, 0)

    COL_PHASES = (0, 2, 3, 6)

    def col_peer(i):
        return lax.rem(c + i, N)

    def row_peer(i):
        return lax.rem(r + i, N)

    def rows_at(ref, at, rows):
        return ref.at[pl.ds(pl.multiple_of(at * rows, rows), rows)]

    def arrived(phase, ref):
        pltpu.make_async_copy(ref, ref, recv_sem.at[phase]).wait()

    qbd[...] = jnp.zeros_like(qbd)
    loads[0].wait()
    query = q_v[...].astype(F32)
    for t in range(2):
        mine = jnp.where(s == 0, query[t, 0:1, :], query[t, 1:2, :])
        for h in range(KV * 8):
            g = h // 8
            one_head = mine[:, h * HD : (h + 1) * HD]
            qbd[2 * h + t : 2 * h + t + 1, g * HD : (g + 1) * HD] = one_head
            heads[h // 2, 2 * (h % 2) + t : 2 * (h % 2) + t + 1, :] = one_head
    loads[1].wait()
    loads[11].wait()
    scale = 1.0 / math.sqrt(HD)
    scores = (
        lax.dot_general(
            qbd[...].astype(BF16), k_v[...], (((1,), (1,)), ((), ())), preferred_element_type=F32
        )
        * scale
    )
    live = c * SPAN + lax.broadcasted_iota(jnp.int32, scores.shape, 1) < len_ref[s]
    scores = jnp.where(live, scores, VERY_LOW)
    peak = jnp.max(scores, axis=1, keepdims=True)
    weights = jnp.where(live, jnp.exp(scores - peak), 0.0)
    total = jnp.sum(weights, axis=1, keepdims=True)
    loads[2].wait()
    summed = jnp.dot(weights.astype(BF16), v_v[...], preferred_element_type=F32)
    low_lane = lax.broadcasted_iota(jnp.int32, (64, HD), 1) < HD // 2
    stats = jnp.where(low_lane, peak, total)
    for o in range(N):
        g = o // 4
        st_a[8 * o : 8 * o + 4, :] = summed[4 * o : 4 * o + 4, g * HD : (g + 1) * HD]
        st_a[8 * o + 4 : 8 * o + 8, :] = stats[4 * o : 4 * o + 4, :]

    met_columns()
    exchange(0, lambda peer: rows_at(st_a, peer, 8), rows_at(rc_a, c, 8), col_peer)
    rows_at(rc_a, c, 8)[...] = rows_at(st_a, c, 8)[...]

    group_lanes = pl.ds(pl.multiple_of((c // 4) * HD, HD), HD)
    for copy in loads[3:8]:
        copy.wait()
    q4 = heads[c]
    fresh_k = nk_v[:, :, group_lanes].astype(F32)
    fresh_v = nv_v[:, :, group_lanes].astype(F32)
    nk = [jnp.where(s == 0, fresh_k[t, 0:1, :], fresh_k[t, 1:2, :]) for t in range(2)]
    nv = [jnp.where(s == 0, fresh_v[t, 0:1, :], fresh_v[t, 1:2, :]) for t in range(2)]
    second = lax.rem(lax.broadcasted_iota(jnp.int32, (4, HD), 0), 2) == 1
    f0 = jnp.broadcast_to(jnp.sum(q4 * nk[0], axis=1, keepdims=True) * scale, (4, HD))
    f1 = jnp.broadcast_to(jnp.sum(q4 * nk[1], axis=1, keepdims=True) * scale, (4, HD))
    f1 = jnp.where(second, f1, VERY_LOW)
    own_row = lax.broadcasted_iota(jnp.int32, (2 * N, 512), 0) == 2 * c + s
    for t in range(2):
        row = jnp.sum(jnp.where(own_row, res_v[t].astype(F32), 0.0), axis=0, keepdims=True)
        for k in range(4):
            resp[2 * k + t : 2 * k + t + 1, :] = row[:, k * HD : (k + 1) * HD]
    gains = gain_v[...].astype(F32).reshape(1, 512)

    arrived(0, rc_a.at[pl.ds(0, 8 * (N - 1))])
    blocks = rc_a[...].reshape(N, 8, HD)
    sums, stat = blocks[:, 0:4, :], blocks[:, 4:8, :]
    low = lax.broadcasted_iota(jnp.int32, (N, 4, HD), 2) < HD // 2
    turned = pltpu.roll(stat, HD // 2, 2)
    peaks = jnp.where(low, stat, turned)
    totals = jnp.where(low, turned, stat)
    top = jnp.maximum(jnp.max(peaks, axis=0), jnp.maximum(f0, f1))
    share = jnp.exp(peaks - top[None])
    e0 = jnp.exp(f0 - top)
    e1 = jnp.where(second, jnp.exp(f1 - top), 0.0)
    whole = jnp.sum(share * totals, axis=0) + e0 + e1
    mixed = jnp.sum(share * sums, axis=0) + e0 * nv[0] + e1 * nv[1]
    st_b[...] = (mixed / whole).astype(BF16).astype(F32)

    met_rows()
    exchange(1, lambda peer: st_b, rc_b.at[r], row_peer)
    rc_b[r] = st_b[...]
    arrived(1, rc_b.at[pl.ds(0, N - 1)])

    def gather(ref, count, stride):
        return jnp.concatenate(
            [
                jnp.concatenate(
                    [ref[pl.ds(2 * k + t, N, stride=stride), :] for k in range(count)], axis=1
                )
                for t in range(2)
            ],
            axis=0,
        )

    def scatter(ref, value, count, stride, base=0):
        for t in range(2):
            for k in range(count):
                ref[pl.ds(base + 2 * k + t, N, stride=stride), :] = value[
                    N * t : N * (t + 1), k * HD : (k + 1) * HD
                ]

    attended = jnp.concatenate(
        [jnp.concatenate([rc_b[:, 2 * j + t, :] for j in range(2)], axis=1) for t in range(2)], axis=0
    )
    part = jnp.dot(attended.astype(BF16), ow_v[...], preferred_element_type=F32)
    scatter(st_c, part, 4, 8)
    exchange(2, lambda peer: rows_at(st_c, peer, 8), rows_at(rc_c, c, 8), col_peer)
    rows_at(rc_c, c, 8)[...] = rows_at(st_c, c, 8)[...]
    arrived(2, rc_c.at[pl.ds(0, 8 * (N - 1))])
    mid_piece = resp[...] + jnp.sum(rc_c[...].reshape(N, 8, HD), axis=0)

    st_d[...] = mid_piece
    exchange(3, lambda peer: st_d, rows_at(rc_d, c, 8), col_peer)
    rows_at(rc_d, c, 8)[...] = st_d[...]
    arrived(3, rc_d.at[pl.ds(0, 8 * (N - 1))])
    mid = gather(rc_d, 4, 8)
    lifted = (mid * gains).astype(BF16)
    squares = jnp.broadcast_to(jnp.sum(mid * mid, axis=1, keepdims=True), (2 * N, HD))
    squares_high = squares.astype(BF16).astype(F32)
    scatter(st_e32, squares_high, 1, 32, 14)
    scatter(st_e32, squares - squares_high, 1, 32, 30)
    loads[8].wait()
    scatter(st_e32, jnp.dot(lifted, gw_v[...], preferred_element_type=F32), 7, 32)
    loads[9].wait()
    scatter(st_e32, jnp.dot(lifted, uw_v[...], preferred_element_type=F32), 7, 32, 16)
    st_e[...] = st_e32[...].astype(BF16)
    exchange(4, lambda peer: rows_at(st_e, peer, 32), rows_at(rc_e, r, 32), row_peer)
    rows_at(rc_e, r, 32)[...] = rows_at(st_e, r, 32)[...]
    arrived(4, rc_e.at[pl.ds(0, 32 * (N - 1))])
    lifts = jnp.sum(rc_e[...].astype(F32).reshape(N, 32, HD), axis=0)
    gate, up = lifts[0:16], lifts[16:32]
    inv0 = lax.rsqrt((gate[14:15] + up[14:15]) / D + 1e-05)
    inv1 = lax.rsqrt((gate[15:16] + up[15:16]) / D + 1e-05)
    odd = lax.rem(lax.broadcasted_iota(jnp.int32, (16, HD), 0), 2) == 1
    inv = jnp.where(odd, inv1, inv0)
    gate, up = gate * inv, up * inv
    st_f[...] = (gate / (1.0 + jnp.exp(-gate)) * up).astype(BF16)

    exchange(5, lambda peer: st_f, rows_at(rc_f, r, 16), row_peer)
    rows_at(rc_f, r, 16)[...] = st_f[...]
    loads[10].wait()
    arrived(5, rc_f.at[pl.ds(0, 16 * (N - 1))])
    f32f[...] = rc_f[...].astype(F32)
    act = gather(f32f, 7, 16).astype(BF16)
    scatter(st_g, jnp.dot(act, dw_v[...], preferred_element_type=F32), 4, 8)
    exchange(6, lambda peer: rows_at(st_g, peer, 8), rows_at(rc_g, c, 8), col_peer)
    rows_at(rc_g, c, 8)[...] = rows_at(st_g, c, 8)[...]
    arrived(6, rc_g.at[pl.ds(0, 8 * (N - 1))])
    st_h[...] = (st_d[...] + jnp.sum(rc_g[...].reshape(N, 8, HD), axis=0)).astype(BF16)

    here = s * N + c

    def give(i, _):
        other = lax.rem(here + i, 2 * N)
        pltpu.make_async_remote_copy(
            src_ref=st_h,
            dst_ref=out_ref.at[here],
            send_sem=send_sem.at[7],
            recv_sem=recv_sem.at[7],
            device_id=(other // N, r, lax.rem(other, N)),
            device_id_type=MESH,
        ).start()
        return 0

    lax.fori_loop(1, 2 * N, give, 0)
    out_ref[here] = st_h[...]

    def sent(phase, ref):
        pltpu.make_async_copy(ref, ref, send_sem.at[phase]).wait()

    sent(0, rc_a.at[pl.ds(0, 8 * (N - 1))])
    sent(1, rc_b.at[pl.ds(0, N - 1)])
    sent(2, rc_c.at[pl.ds(0, 8 * (N - 1))])
    sent(3, rc_d.at[pl.ds(0, 8 * (N - 1))])
    sent(4, rc_e.at[pl.ds(0, 32 * (N - 1))])
    sent(5, rc_f.at[pl.ds(0, 16 * (N - 1))])
    sent(6, rc_g.at[pl.ds(0, 8 * (N - 1))])
    arrived(7, out_ref.at[pl.ds(0, 2 * N - 1)])
    sent(7, out_ref.at[pl.ds(0, 2 * N - 1)])


def shards(query, new_keys, new_values, key_cache, value_cache, lengths, residual, out_weight,
           norm_gain, gate_weight, up_weight, down_weight):
    def vm(*shape, kind=F32):
        return pltpu.VMEM(shape, kind)

    hbm = pl.BlockSpec(memory_space=pltpu.HBM)
    pieces = pl.pallas_call(
        kernel,
        out_shape=jax.ShapeDtypeStruct((2 * N, 8, HD), BF16),
        in_specs=[hbm] * 12,
        out_specs=pl.BlockSpec(memory_space=pltpu.VMEM),
        scratch_shapes=[
            pltpu.SMEM((2,), jnp.int32),
            vm(2, 2, 4096, kind=BF16),
            vm(2, 2, 512, kind=BF16),
            vm(2, 2, 512, kind=BF16),
            vm(SPAN, 512, kind=BF16),
            vm(SPAN, 512, kind=BF16),
            vm(2, 32, 512, kind=BF16),
            vm(256, 512, kind=BF16),
            vm(512, kind=BF16),
            vm(512, 896, kind=BF16),
            vm(512, 896, kind=BF16),
            vm(896, 512, kind=BF16),
            vm(64, 512),
            vm(N, 4, HD),
            vm(8, HD),
            vm(8 * N, HD), vm(8 * N, HD),
            vm(4, HD), vm(N, 4, HD),
            vm(8 * N, HD), vm(8 * N, HD),
            vm(8, HD), vm(8 * N, HD),
            vm(32 * N, HD), vm(32 * N, HD, kind=BF16), vm(32 * N, HD, kind=BF16),
            vm(16, HD, kind=BF16), vm(16 * N, HD, kind=BF16), vm(16 * N, HD),
            vm(8 * N, HD), vm(8 * N, HD),
            vm(8, HD, kind=BF16),
            pltpu.SemaphoreType.DMA((12,)),
            pltpu.SemaphoreType.DMA((8,)),
            pltpu.SemaphoreType.DMA((8,)),
            pltpu.SemaphoreType.REGULAR,
        ],
        compiler_params=pltpu.CompilerParams(
            collective_id=0, has_side_effects=True, vmem_limit_bytes=32 * 1024 * 1024
        ),
        name="layer",
    )(*[
        pltpu.with_memory_space_constraint(a, pltpu.HBM)
        for a in (lengths, query, new_keys, new_values, key_cache, value_cache, residual, out_weight,
                  norm_gain, gate_weight, up_weight, down_weight)
    ])
    pieces = pieces.reshape(2, N, 4, 2, HD)
    return pieces.transpose(3, 1, 0, 2, 4).reshape(2, 2 * N, 512)


def solution(mesh):
    in_specs = (
        P(None, "row", None),
        P(None, "row", None),
        P(None, "row", None),
        P("row", "col", None),
        P("row", "col", None),
        P("row"),
        P(None, None, "row"),
        P("col", "row"),
        P("row"),
        P("row", "col"),
        P("row", "col"),
        P("col", "row"),
    )
    out_specs = P(None, None, "row")
    return jax.shard_map(shards, mesh=mesh, in_specs=in_specs, out_specs=out_specs, check_vma=False)
```

```python
import functools
import math

import jax
import jax.numpy as jnp
from jax import lax
from jax.experimental import pallas as pl
from jax.experimental.pallas import tpu as pltpu
from jax.sharding import PartitionSpec as P

D = 8192
KV = 4
HD = 128
N = 16
SPAN = 384
VERY_LOW = -1e30
F32 = jnp.float32
BF16 = jnp.bfloat16
MESH = pl.DeviceIdType.MESH


def kernel(
    len_hbm, q_hbm, nk_hbm, nv_hbm, k_hbm, v_hbm, res_hbm, ow_hbm, gain_hbm, gw_hbm, uw_hbm, dw_hbm,
    out_ref,
    len_ref, q_v, nk_v, nv_v, k_v, v_v, res_v, ow_v, gain_v, gw_v, uw_v, dw_v,
    qbd, heads, res_s, mid_t,
    st_a, rc_a, st_b, rc_b, st_c, rc_c, st_e32, st_e, rc_e, st_f, rc_f, f32f, st_g, rc_g, st_h,
    load_sem, send_sem, recv_sem, met_sem,
):
    s = lax.axis_index("side")
    r = lax.axis_index("row")
    c = lax.axis_index("col")

    barrier = pltpu.get_barrier_semaphore()

    odd = lax.rem(c, 2)

    def greet_row(i, _):
        pl.semaphore_signal(
            barrier,
            inc=1,
            device_id=(s, lax.rem(r + N // 2 + (i + 1) // 2 * (1 - 2 * lax.rem(i, 2)), N), c - odd + 1),
            device_id_type=MESH,
        )
        return 0

    def greet_col(i, _):
        other = lax.rem(s * N + c + odd + i, 2 * N)
        pl.semaphore_signal(
            barrier, inc=1, device_id=(other // N, r, lax.rem(other, N)), device_id_type=MESH
        )
        return 0

    lax.fori_loop(0, N - 1, greet_row, 0)
    lax.fori_loop(1, N, lambda i, _: greet_col(2 * i, 0), 0)

    @pl.when(odd == 1)
    def _():
        greet_col(0, 0)

    @pl.when(odd == 0)
    def _():
        pl.semaphore_signal(barrier, inc=1, device_id=(s, r, c + 1), device_id_type=MESH)

    loads = [
        pltpu.make_async_copy(src, dst, load_sem.at[i])
        for i, (src, dst) in enumerate(
            [
                (q_hbm, q_v),
                (k_hbm.at[s], k_v),
                (v_hbm.at[s], v_v),
                (nk_hbm, nk_v),
                (nv_hbm, nv_v),
                (res_hbm, res_v),
                (gain_hbm, gain_v),
                (ow_hbm, ow_v),
                (gw_hbm, gw_v),
                (uw_hbm, uw_v),
                (dw_hbm, dw_v),
                (len_hbm, len_ref),
            ]
        )
    ]
    for copy in loads:
        copy.start()

    def met_columns():
        @pl.when(odd == 0)
        def _():
            pl.semaphore_wait(barrier, 2 * N - 1)
            pl.semaphore_signal(met_sem, inc=1, device_id=(s, r, c + 1), device_id_type=MESH)

        @pl.when(odd == 1)
        def _():
            pl.semaphore_wait(met_sem, 1)

    def met_rows():
        @pl.when(odd == 1)
        def _():
            pl.semaphore_wait(barrier, 2 * N - 1)
            pl.semaphore_signal(met_sem, inc=1, device_id=(s, r, c - 1), device_id_type=MESH)

        @pl.when(odd == 0)
        def _():
            pl.semaphore_wait(met_sem, 1)

    def rows_at(ref, at, rows):
        return ref.at[pl.ds(pl.multiple_of(at * rows, rows), rows)]

    def offset(p):
        half = (p + 1) // 2
        return N + half * (2 * lax.rem(p, 2) - 1)

    def place(o):
        return jnp.where(o == 0, 0, jnp.where(o <= N // 2, 2 * o - 1, 2 * (N - o)))

    def send(phase, source, target, device):
        pltpu.make_async_remote_copy(
            src_ref=source,
            dst_ref=target,
            send_sem=send_sem.at[phase],
            recv_sem=recv_sem.at[phase],
            device_id=device,
            device_id_type=MESH,
        ).start()

    def each(first, last, step):
        def one(i, _):
            step(i)
            return 0

        lax.fori_loop(first, last, one, 0)

    def to_columns(phase, source, target):
        def one(i):
            half = (i + 1) // 2
            peer = lax.rem(c + N // 2 + half * (1 - 2 * lax.rem(i, 2)), N)
            send(phase, source(peer), target, (s, r, peer))

        each(0, N - 1, one)

    def arrived(phase, ref):
        pltpu.make_async_copy(ref, ref, recv_sem.at[phase]).wait()

    def sent(phase, ref):
        pltpu.make_async_copy(ref, ref, send_sem.at[phase]).wait()

    qbd[...] = jnp.zeros_like(qbd)
    loads[0].wait()
    query = q_v[...].astype(F32)
    for t in range(2):
        mine = jnp.where(s == 0, query[t, 0:1, :], query[t, 1:2, :])
        for h in range(KV * 8):
            g = h // 8
            one_head = mine[:, h * HD : (h + 1) * HD]
            qbd[2 * h + t : 2 * h + t + 1, g * HD : (g + 1) * HD] = one_head
            heads[h // 2, 2 * (h % 2) + t : 2 * (h % 2) + t + 1, :] = one_head
    loads[1].wait()
    loads[11].wait()
    scale = 1.0 / math.sqrt(HD)
    scores = (
        lax.dot_general(
            qbd[...].astype(BF16), k_v[...], (((1,), (1,)), ((), ())), preferred_element_type=F32
        )
        * scale
    )
    live = c * SPAN + lax.broadcasted_iota(jnp.int32, scores.shape, 1) < len_ref[s]
    scores = jnp.where(live, scores, VERY_LOW)
    peak = jnp.max(scores, axis=1, keepdims=True)
    weights = jnp.where(live, jnp.exp(scores - peak), 0.0)
    total = jnp.sum(weights, axis=1, keepdims=True)
    loads[2].wait()
    summed = jnp.dot(weights.astype(BF16), v_v[...], preferred_element_type=F32)
    low_lane = lax.broadcasted_iota(jnp.int32, (64, HD), 1) < HD // 2
    stats = jnp.where(low_lane, peak, total)
    for o in range(N):
        g = o // 4
        st_a[8 * o : 8 * o + 4, :] = summed[4 * o : 4 * o + 4, g * HD : (g + 1) * HD]
        st_a[8 * o + 4 : 8 * o + 8, :] = stats[4 * o : 4 * o + 4, :]

    met_columns()
    to_columns(0, lambda peer: rows_at(st_a, peer, 8), rows_at(rc_a, c, 8))
    rows_at(rc_a, c, 8)[...] = rows_at(st_a, c, 8)[...]

    group_lanes = pl.ds(pl.multiple_of((c // 4) * HD, HD), HD)
    for copy in loads[3:8]:
        copy.wait()
    q4 = heads[c]
    fresh_k = nk_v[:, :, group_lanes].astype(F32)
    fresh_v = nv_v[:, :, group_lanes].astype(F32)
    nk = [jnp.where(s == 0, fresh_k[t, 0:1, :], fresh_k[t, 1:2, :]) for t in range(2)]
    nv = [jnp.where(s == 0, fresh_v[t, 0:1, :], fresh_v[t, 1:2, :]) for t in range(2)]
    second = lax.rem(lax.broadcasted_iota(jnp.int32, (4, HD), 0), 2) == 1
    f0 = jnp.broadcast_to(jnp.sum(q4 * nk[0], axis=1, keepdims=True) * scale, (4, HD))
    f1 = jnp.broadcast_to(jnp.sum(q4 * nk[1], axis=1, keepdims=True) * scale, (4, HD))
    f1 = jnp.where(second, f1, VERY_LOW)
    at = lax.broadcasted_iota(jnp.int32, (2 * N, 4 * N), 0)
    other = lax.rem(r + offset(at // N * 8 + lax.rem(at, 8)), N)
    wanted = lax.rem(at // 8, 2) * 2 * N + 2 * other + s
    chosen = lax.broadcasted_iota(jnp.int32, (2 * N, 4 * N), 1) == wanted
    res_s[...] = jnp.dot(
        jnp.where(chosen, 1.0, 0.0).astype(BF16), res_v[...].reshape(4 * N, 512), preferred_element_type=F32
    )
    gains = gain_v[...].astype(F32).reshape(1, 512)

    arrived(0, rc_a.at[pl.ds(0, 8 * (N - 1))])
    blocks = rc_a[...].reshape(N, 8, HD)
    sums, stat = blocks[:, 0:4, :], blocks[:, 4:8, :]
    low = lax.broadcasted_iota(jnp.int32, (N, 4, HD), 2) < HD // 2
    turned = pltpu.roll(stat, HD // 2, 2)
    peaks = jnp.where(low, stat, turned)
    totals = jnp.where(low, turned, stat)
    top = jnp.maximum(jnp.max(peaks, axis=0), jnp.maximum(f0, f1))
    share = jnp.exp(peaks - top[None])
    e0 = jnp.exp(f0 - top)
    e1 = jnp.where(second, jnp.exp(f1 - top), 0.0)
    whole = jnp.sum(share * totals, axis=0) + e0 + e1
    mixed = jnp.sum(share * sums, axis=0) + e0 * nv[0] + e1 * nv[1]
    st_b[...] = (mixed / whole).astype(BF16).astype(F32)

    met_rows()
    def give_attended(near):
        def one(i):
            p = (8 if near else N) - 1 - i
            send(1 if near else 2, st_b, rc_b.at[p], (s, lax.rem(r + 2 * N - offset(p), N), c))

        each(0, 7 if near else 8, one)

    give_attended(False)
    give_attended(True)
    rc_b[0] = st_b[...]

    def project(k):
        near = rc_b.at[pl.ds(8 * k, 8)]
        attended = jnp.concatenate(
            [jnp.concatenate([near[:, 2 * j + t, :] for j in range(2)], axis=1) for t in range(2)], axis=0
        )
        st_c[k] = jnp.dot(attended.astype(BF16), ow_v[...], preferred_element_type=F32).astype(BF16)
        to_columns(3 + k, lambda peer: st_c.at[k], rc_c.at[k, c])
        rc_c[k, c] = st_c[k]

    def lift(k):
        mid = res_s[N * k : N * (k + 1), :] + jnp.sum(rc_c[k].astype(F32), axis=0)
        lifted = (mid * gains).astype(BF16)
        squares = jnp.broadcast_to(jnp.sum(mid * mid, axis=1, keepdims=True), (N, HD))
        high = squares.astype(BF16).astype(F32)
        scatter(st_e32, high, 1, 32, 256 * k + 14)
        scatter(st_e32, squares - high, 1, 32, 256 * k + 30)
        if k == 0:
            loads[8].wait()
        scatter(st_e32, jnp.dot(lifted, gw_v[...], preferred_element_type=F32), 7, 32, 256 * k)
        if k == 0:
            loads[9].wait()
        scatter(st_e32, jnp.dot(lifted, uw_v[...], preferred_element_type=F32), 7, 32, 256 * k + 16)
        st_e[256 * k : 256 * (k + 1), :] = st_e32[256 * k : 256 * (k + 1), :].astype(BF16)

        def one(p):
            owner = lax.rem(r + N // 2 + offset(p), N)
            send(5, rows_at(st_e, p, 32), rows_at(rc_e, p, 32), (s, owner, c))

        each(8 * k, 8 + 7 * k, one)
        scatter(mid_t, mid, 4, 8, 64 * k)

    def scatter(ref, value, count, stride, base):
        for t in range(2):
            for m in range(count):
                ref[pl.ds(base + 2 * m + t, 8, stride=stride), :] = value[
                    8 * t : 8 * (t + 1), m * HD : (m + 1) * HD
                ]

    arrived(1, rc_b.at[pl.ds(0, 7)])
    project(0)
    arrived(2, rc_b.at[pl.ds(0, 8)])
    project(1)
    arrived(3, rc_c.at[0, pl.ds(0, N - 1)])
    lift(0)
    arrived(4, rc_c.at[1, pl.ds(0, N - 1)])
    lift(1)
    rc_e[32 * (N - 1) :, :] = st_e[32 * (N - 1) :, :]
    arrived(5, rc_e.at[pl.ds(0, 32 * (N - 1))])
    lifts = jnp.sum(rc_e[...].astype(F32).reshape(N, 32, HD), axis=0)
    gate, up = lifts[0:16], lifts[16:32]
    inv0 = lax.rsqrt((gate[14:15] + up[14:15]) / D + 1e-05)
    inv1 = lax.rsqrt((gate[15:16] + up[15:16]) / D + 1e-05)
    inv = jnp.where(lax.rem(lax.broadcasted_iota(jnp.int32, (16, HD), 0), 2) == 1, inv1, inv0)
    gate, up = gate * inv, up * inv
    st_f[...] = (gate / (1.0 + jnp.exp(-gate)) * up).astype(BF16)

    def give_act(i):
        p = N - 1 - i
        send(6, st_f, rows_at(rc_f, p, 16), (s, lax.rem(r + 2 * N - offset(p), N), c))

    each(0, N - 1, give_act)
    rc_f[0:16, :] = st_f[...]
    loads[10].wait()
    arrived(6, rc_f.at[pl.ds(0, 16 * (N - 1))])
    f32f[...] = rc_f[...].astype(F32)
    act = jnp.concatenate(
        [
            jnp.concatenate([f32f[pl.ds(2 * m + t, N, stride=16), :] for m in range(7)], axis=1)
            for t in range(2)
        ],
        axis=0,
    )
    part = jnp.dot(act.astype(BF16), dw_v[...], preferred_element_type=F32)
    for t in range(2):
        for m in range(4):
            st_g[pl.ds(2 * m + t, N, stride=8), :] = part[N * t : N * (t + 1), m * HD : (m + 1) * HD]

    def act_place(row):
        return place(lax.rem(row + N + N // 2 - r, N))

    to_columns(7, lambda peer: rows_at(st_g, act_place(peer), 8), rows_at(rc_g, c, 8))
    rows_at(rc_g, c, 8)[...] = rows_at(st_g, act_place(c), 8)[...]
    arrived(7, rc_g.at[pl.ds(0, 8 * (N - 1))])
    mid_piece = rows_at(mid_t, place(lax.rem(c + N - r, N)), 8)[...]
    st_h[...] = (mid_piece + jnp.sum(rc_g[...].reshape(N, 8, HD), axis=0)).astype(BF16)
    here = s * N + c

    def give(i):
        other = lax.rem(here + i, 2 * N)
        send(8, st_h, out_ref.at[here], (other // N, r, lax.rem(other, N)))

    each(1, 2 * N, give)
    out_ref[here] = st_h[...]

    sent(0, rc_a.at[pl.ds(0, 8 * (N - 1))])
    sent(1, rc_b.at[pl.ds(0, 7)])
    sent(2, rc_b.at[pl.ds(0, 8)])
    sent(3, rc_c.at[0, pl.ds(0, N - 1)])
    sent(4, rc_c.at[1, pl.ds(0, N - 1)])
    sent(5, rc_e.at[pl.ds(0, 32 * (N - 1))])
    sent(6, rc_f.at[pl.ds(0, 16 * (N - 1))])
    sent(7, rc_g.at[pl.ds(0, 8 * (N - 1))])
    arrived(8, out_ref.at[pl.ds(0, 2 * N - 1)])
    sent(8, out_ref.at[pl.ds(0, 2 * N - 1)])


def shards(query, new_keys, new_values, key_cache, value_cache, lengths, residual, out_weight,
           norm_gain, gate_weight, up_weight, down_weight):
    def vm(*shape, kind=F32):
        return pltpu.VMEM(shape, kind)

    hbm = pl.BlockSpec(memory_space=pltpu.HBM)
    pieces = pl.pallas_call(
        kernel,
        out_shape=jax.ShapeDtypeStruct((2 * N, 8, HD), BF16),
        in_specs=[hbm] * 12,
        out_specs=pl.BlockSpec(memory_space=pltpu.VMEM),
        scratch_shapes=[
            pltpu.SMEM((2,), jnp.int32),
            vm(2, 2, 4096, kind=BF16),
            vm(2, 2, 512, kind=BF16),
            vm(2, 2, 512, kind=BF16),
            vm(SPAN, 512, kind=BF16),
            vm(SPAN, 512, kind=BF16),
            vm(2, 32, 512, kind=BF16),
            vm(256, 512, kind=BF16),
            vm(512, kind=BF16),
            vm(512, 896, kind=BF16),
            vm(512, 896, kind=BF16),
            vm(896, 512, kind=BF16),
            vm(64, 512),
            vm(N, 4, HD),
            vm(2 * N, 512),
            vm(8 * N, HD),
            vm(8 * N, HD), vm(8 * N, HD),
            vm(4, HD), vm(N, 4, HD),
            vm(2, N, 512, kind=BF16), vm(2, N, N, 512, kind=BF16),
            vm(32 * N, HD), vm(32 * N, HD, kind=BF16), vm(32 * N, HD, kind=BF16),
            vm(16, HD, kind=BF16), vm(16 * N, HD, kind=BF16), vm(16 * N, HD),
            vm(8 * N, HD), vm(8 * N, HD),
            vm(8, HD, kind=BF16),
            pltpu.SemaphoreType.DMA((12,)),
            pltpu.SemaphoreType.DMA((9,)),
            pltpu.SemaphoreType.DMA((9,)),
            pltpu.SemaphoreType.REGULAR,
        ],
        compiler_params=pltpu.CompilerParams(
            collective_id=0, has_side_effects=True, vmem_limit_bytes=32 * 1024 * 1024
        ),
        name="layer",
    )(*[
        pltpu.with_memory_space_constraint(a, pltpu.HBM)
        for a in (lengths, query, new_keys, new_values, key_cache, value_cache, residual, out_weight,
                  norm_gain, gate_weight, up_weight, down_weight)
    ])
    pieces = pieces.reshape(2, N, 4, 2, HD)
    return pieces.transpose(3, 1, 0, 2, 4).reshape(2, 2 * N, 512)


def solution(mesh):
    in_specs = (
        P(None, "row", None),
        P(None, "row", None),
        P(None, "row", None),
        P("row", "col", None),
        P("row", "col", None),
        P("row"),
        P(None, None, "row"),
        P("col", "row"),
        P("row"),
        P("row", "col"),
        P("row", "col"),
        P("col", "row"),
    )
    out_specs = P(None, None, "row")
    return jax.shard_map(shards, mesh=mesh, in_specs=in_specs, out_specs=out_specs, check_vma=False)
```

```python
import functools
import math

import jax
import jax.numpy as jnp
from jax import lax
from jax.experimental import pallas as pl
from jax.experimental.pallas import tpu as pltpu
from jax.sharding import PartitionSpec as P

D = 8192
KV = 4
HD = 128
N = 16
SPAN = 384
VERY_LOW = -1e30
F32 = jnp.float32
BF16 = jnp.bfloat16
MESH = pl.DeviceIdType.MESH


def kernel(
    len_hbm, q_hbm, nk_hbm, nv_hbm, k_hbm, v_hbm, res_hbm, ow_hbm, gain_hbm, gw_hbm, uw_hbm, dw_hbm,
    out_ref,
    len_ref, q_v, nk_v, nv_v, k_v, v_v, res_v, ow_v, gain_v, gw_v, uw_v, dw_v,
    qbd, heads, res_s, mid_t,
    st_a, rc_a, st_b, rc_b, st_c, rc_c, st_e32, st_e, rc_e, st_f, rc_f, f32f, st_g, rc_g, st_h,
    load_sem, send_sem, recv_sem, met_sem,
):
    s = lax.axis_index("side")
    r = lax.axis_index("row")
    c = lax.axis_index("col")

    barrier = pltpu.get_barrier_semaphore()

    odd = lax.rem(c, 2)

    def greet_row(i, _):
        pl.semaphore_signal(
            barrier,
            inc=1,
            device_id=(s, lax.rem(r + N // 2 + (i + 1) // 2 * (1 - 2 * lax.rem(i, 2)), N), c - odd + 1),
            device_id_type=MESH,
        )
        return 0

    def greet_col(i, _):
        pl.semaphore_signal(
            barrier, inc=1, device_id=(s, r, lax.rem(c + odd + 2 * i, N)), device_id_type=MESH
        )
        return 0

    def greet_side(i, _):
        pl.semaphore_signal(barrier, inc=1, device_id=(1 - s, r, 2 * i + 1), device_id_type=MESH)
        return 0

    lax.fori_loop(0, N - 1, greet_row, 0)

    @pl.when(odd == 1)
    def _():
        greet_col(0, 0)

    lax.fori_loop(1, N // 2, greet_col, 0)

    @pl.when(odd == 0)
    def _():
        pl.semaphore_signal(barrier, inc=1, device_id=(s, r, c + 1), device_id_type=MESH)

    lax.fori_loop(0, N // 2, greet_side, 0)

    loads = [
        pltpu.make_async_copy(src, dst, load_sem.at[i])
        for i, (src, dst) in enumerate(
            [
                (q_hbm, q_v),
                (k_hbm.at[s], k_v),
                (v_hbm.at[s], v_v),
                (nk_hbm, nk_v),
                (nv_hbm, nv_v),
                (res_hbm, res_v),
                (gain_hbm, gain_v),
                (ow_hbm, ow_v),
                (gw_hbm, gw_v),
                (uw_hbm, uw_v),
                (dw_hbm, dw_v),
                (len_hbm, len_ref),
            ]
        )
    ]
    for copy in loads:
        copy.start()

    def met_columns():
        @pl.when(odd == 0)
        def _():
            pl.semaphore_wait(barrier, N - 1)
            pl.semaphore_signal(met_sem, inc=1, device_id=(s, r, c + 1), device_id_type=MESH)

        @pl.when(odd == 1)
        def _():
            pl.semaphore_wait(met_sem, 1)

    def met_rows():
        @pl.when(odd == 1)
        def _():
            pl.semaphore_wait(barrier, 3 * N - 1)
            pl.semaphore_signal(met_sem, inc=1, device_id=(s, r, c - 1), device_id_type=MESH)

        @pl.when(odd == 0)
        def _():
            pl.semaphore_wait(met_sem, 1)

    def rows_at(ref, at, rows):
        return ref.at[pl.ds(pl.multiple_of(at * rows, rows), rows)]

    def offset(p):
        half = (p + 1) // 2
        return N + half * (2 * lax.rem(p, 2) - 1)

    def place(o):
        return jnp.where(o == 0, 0, jnp.where(o <= N // 2, 2 * o - 1, 2 * (N - o)))

    def send(phase, source, target, device):
        pltpu.make_async_remote_copy(
            src_ref=source,
            dst_ref=target,
            send_sem=send_sem.at[phase],
            recv_sem=recv_sem.at[phase],
            device_id=device,
            device_id_type=MESH,
        ).start()

    def each(first, last, step):
        def one(i, _):
            step(i)
            return 0

        lax.fori_loop(first, last, one, 0)

    def to_columns(phase, source, target):
        def one(i):
            half = (i + 1) // 2
            peer = lax.rem(c + N // 2 + half * (1 - 2 * lax.rem(i, 2)), N)
            send(phase, source(peer), target, (s, r, peer))

        each(0, N - 1, one)

    def arrived(phase, ref):
        pltpu.make_async_copy(ref, ref, recv_sem.at[phase]).wait()

    def sent(phase, ref):
        pltpu.make_async_copy(ref, ref, send_sem.at[phase]).wait()

    qbd[...] = jnp.zeros_like(qbd)
    loads[0].wait()
    query = q_v[...].astype(F32)
    for t in range(2):
        mine = jnp.where(s == 0, query[t, 0:1, :], query[t, 1:2, :])
        for h in range(KV * 8):
            g = h // 8
            one_head = mine[:, h * HD : (h + 1) * HD]
            qbd[2 * h + t : 2 * h + t + 1, g * HD : (g + 1) * HD] = one_head
            heads[h // 2, 2 * (h % 2) + t : 2 * (h % 2) + t + 1, :] = one_head
    loads[1].wait()
    loads[11].wait()
    scale = 1.0 / math.sqrt(HD)
    scores = (
        lax.dot_general(
            qbd[...].astype(BF16), k_v[...], (((1,), (1,)), ((), ())), preferred_element_type=F32
        )
        * scale
    )
    live = c * SPAN + lax.broadcasted_iota(jnp.int32, scores.shape, 1) < len_ref[s]
    scores = jnp.where(live, scores, VERY_LOW)
    peak = jnp.max(scores, axis=1, keepdims=True)
    weights = jnp.where(live, jnp.exp(scores - peak), 0.0)
    total = jnp.sum(weights, axis=1, keepdims=True)
    loads[2].wait()
    summed = jnp.dot(weights.astype(BF16), v_v[...], preferred_element_type=F32)
    low_lane = lax.broadcasted_iota(jnp.int32, (64, HD), 1) < HD // 2
    stats = jnp.where(low_lane, peak, total)
    for o in range(N):
        g = o // 4
        st_a[8 * o : 8 * o + 4, :] = summed[4 * o : 4 * o + 4, g * HD : (g + 1) * HD]
        st_a[8 * o + 4 : 8 * o + 8, :] = stats[4 * o : 4 * o + 4, :]

    met_columns()
    to_columns(0, lambda peer: rows_at(st_a, peer, 8), rows_at(rc_a, c, 8))
    rows_at(rc_a, c, 8)[...] = rows_at(st_a, c, 8)[...]

    group_lanes = pl.ds(pl.multiple_of((c // 4) * HD, HD), HD)
    for copy in loads[3:8]:
        copy.wait()
    q4 = heads[c]
    fresh_k = nk_v[:, :, group_lanes].astype(F32)
    fresh_v = nv_v[:, :, group_lanes].astype(F32)
    nk = [jnp.where(s == 0, fresh_k[t, 0:1, :], fresh_k[t, 1:2, :]) for t in range(2)]
    nv = [jnp.where(s == 0, fresh_v[t, 0:1, :], fresh_v[t, 1:2, :]) for t in range(2)]
    second = lax.rem(lax.broadcasted_iota(jnp.int32, (4, HD), 0), 2) == 1
    f0 = jnp.broadcast_to(jnp.sum(q4 * nk[0], axis=1, keepdims=True) * scale, (4, HD))
    f1 = jnp.broadcast_to(jnp.sum(q4 * nk[1], axis=1, keepdims=True) * scale, (4, HD))
    f1 = jnp.where(second, f1, VERY_LOW)
    at = lax.broadcasted_iota(jnp.int32, (2 * N, 4 * N), 0)
    other = lax.rem(r + offset(at // 8 * 4 + lax.rem(at, 4)), N)
    wanted = lax.rem(at // 4, 2) * 2 * N + 2 * other + s
    chosen = lax.broadcasted_iota(jnp.int32, (2 * N, 4 * N), 1) == wanted
    res_s[...] = jnp.dot(
        jnp.where(chosen, 1.0, 0.0).astype(BF16), res_v[...].reshape(4 * N, 512), preferred_element_type=F32
    )
    gains = gain_v[...].astype(F32).reshape(1, 512)

    arrived(0, rc_a.at[pl.ds(0, 8 * (N - 1))])
    blocks = rc_a[...].reshape(N, 8, HD)
    sums, stat = blocks[:, 0:4, :], blocks[:, 4:8, :]
    low = lax.broadcasted_iota(jnp.int32, (N, 4, HD), 2) < HD // 2
    turned = pltpu.roll(stat, HD // 2, 2)
    peaks = jnp.where(low, stat, turned)
    totals = jnp.where(low, turned, stat)
    top = jnp.maximum(jnp.max(peaks, axis=0), jnp.maximum(f0, f1))
    share = jnp.exp(peaks - top[None])
    e0 = jnp.exp(f0 - top)
    e1 = jnp.where(second, jnp.exp(f1 - top), 0.0)
    whole = jnp.sum(share * totals, axis=0) + e0 + e1
    mixed = jnp.sum(share * sums, axis=0) + e0 * nv[0] + e1 * nv[1]
    st_b[...] = (mixed / whole).astype(BF16).astype(F32)

    met_rows()
    def give_attended(k):
        def one(i):
            p = 4 * k + 3 - i
            send(1 + k, st_b, rc_b.at[p], (s, lax.rem(r + 2 * N - offset(p), N), c))

        each(0, 4 if k else 3, one)

    for k in range(3, -1, -1):
        give_attended(k)
    rc_b[0] = st_b[...]

    def project(k):
        attended = jnp.concatenate(
            [
                jnp.concatenate([rc_b[4 * k : 4 * k + 4, 2 * j + t, :] for j in range(2)], axis=1)
                for t in range(2)
            ],
            axis=0,
        )
        st_c[k] = jnp.dot(attended.astype(BF16), ow_v[...], preferred_element_type=F32).astype(BF16)
        to_columns(5 + k, lambda peer: st_c.at[k], rc_c.at[k, c])
        rc_c[k, c] = st_c[k]

    def scatter(ref, value, count, stride, base):
        for t in range(2):
            for m in range(count):
                ref[pl.ds(base + 2 * m + t, 4, stride=stride), :] = value[
                    4 * t : 4 * (t + 1), m * HD : (m + 1) * HD
                ]

    def lift(k):
        mid = res_s[8 * k : 8 * (k + 1), :] + jnp.sum(rc_c[k].astype(F32), axis=0)
        lifted = (mid * gains).astype(BF16)
        squares = jnp.broadcast_to(jnp.sum(mid * mid, axis=1, keepdims=True), (8, HD))
        high = squares.astype(BF16).astype(F32)
        base = 128 * k
        scatter(st_e32, high, 1, 32, base + 14)
        scatter(st_e32, squares - high, 1, 32, base + 30)
        if k == 0:
            loads[8].wait()
        scatter(st_e32, jnp.dot(lifted, gw_v[...], preferred_element_type=F32), 7, 32, base)
        if k == 0:
            loads[9].wait()
        scatter(st_e32, jnp.dot(lifted, uw_v[...], preferred_element_type=F32), 7, 32, base + 16)
        st_e[base : base + 128, :] = st_e32[base : base + 128, :].astype(BF16)

        def one(p):
            owner = lax.rem(r + N // 2 + offset(p), N)
            send(9, rows_at(st_e, p, 32), rows_at(rc_e, p, 32), (s, owner, c))

        each(4 * k, 4 * k + (4 if k < 3 else 3), one)
        scatter(mid_t, mid, 4, 8, 32 * k)

    arrived(1, rc_b.at[pl.ds(0, 3)])
    project(0)
    arrived(2, rc_b.at[pl.ds(0, 4)])
    project(1)
    arrived(3, rc_b.at[pl.ds(0, 4)])
    project(2)
    arrived(4, rc_b.at[pl.ds(0, 4)])
    project(3)
    arrived(5, rc_c.at[0, pl.ds(0, N - 1)])
    lift(0)
    arrived(6, rc_c.at[1, pl.ds(0, N - 1)])
    lift(1)
    arrived(7, rc_c.at[2, pl.ds(0, N - 1)])
    lift(2)
    arrived(8, rc_c.at[3, pl.ds(0, N - 1)])
    lift(3)
    rc_e[32 * (N - 1) :, :] = st_e[32 * (N - 1) :, :]
    arrived(9, rc_e.at[pl.ds(0, 32 * (N - 1))])
    lifts = jnp.sum(rc_e[...].astype(F32).reshape(N, 32, HD), axis=0)
    gate, up = lifts[0:16], lifts[16:32]
    inv0 = lax.rsqrt((gate[14:15] + up[14:15]) / D + 1e-05)
    inv1 = lax.rsqrt((gate[15:16] + up[15:16]) / D + 1e-05)
    inv = jnp.where(lax.rem(lax.broadcasted_iota(jnp.int32, (16, HD), 0), 2) == 1, inv1, inv0)
    gate, up = gate * inv, up * inv
    st_f[...] = (gate / (1.0 + jnp.exp(-gate)) * up).astype(BF16)

    def give_act(i):
        p = N - 1 - i
        send(10, st_f, rows_at(rc_f, p, 16), (s, lax.rem(r + 2 * N - offset(p), N), c))

    each(0, N - 1, give_act)
    rc_f[0:16, :] = st_f[...]
    loads[10].wait()
    arrived(10, rc_f.at[pl.ds(0, 16 * (N - 1))])
    f32f[...] = rc_f[...].astype(F32)
    act = jnp.concatenate(
        [
            jnp.concatenate([f32f[pl.ds(2 * m + t, N, stride=16), :] for m in range(7)], axis=1)
            for t in range(2)
        ],
        axis=0,
    )
    part = jnp.dot(act.astype(BF16), dw_v[...], preferred_element_type=F32)
    for t in range(2):
        for m in range(4):
            st_g[pl.ds(2 * m + t, N, stride=8), :] = part[N * t : N * (t + 1), m * HD : (m + 1) * HD]

    def act_place(row):
        return place(lax.rem(row + N + N // 2 - r, N))

    to_columns(11, lambda peer: rows_at(st_g, act_place(peer), 8), rows_at(rc_g, c, 8))
    rows_at(rc_g, c, 8)[...] = rows_at(st_g, act_place(c), 8)[...]
    arrived(11, rc_g.at[pl.ds(0, 8 * (N - 1))])
    mid_piece = rows_at(mid_t, place(lax.rem(c + N - r, N)), 8)[...]
    st_h[...] = (mid_piece + jnp.sum(rc_g[...].reshape(N, 8, HD), axis=0)).astype(BF16)
    here = s * N + c

    def give(i):
        other = lax.rem(here + i, 2 * N)
        send(12, st_h, out_ref.at[here], (other // N, r, lax.rem(other, N)))

    each(1, 2 * N, give)
    out_ref[here] = st_h[...]

    sent(0, rc_a.at[pl.ds(0, 8 * (N - 1))])
    sent(1, rc_b.at[pl.ds(0, 3)])
    sent(2, rc_b.at[pl.ds(0, 4)])
    sent(3, rc_b.at[pl.ds(0, 4)])
    sent(4, rc_b.at[pl.ds(0, 4)])
    sent(5, rc_c.at[0, pl.ds(0, N - 1)])
    sent(6, rc_c.at[1, pl.ds(0, N - 1)])
    sent(7, rc_c.at[2, pl.ds(0, N - 1)])
    sent(8, rc_c.at[3, pl.ds(0, N - 1)])
    sent(9, rc_e.at[pl.ds(0, 32 * (N - 1))])
    sent(10, rc_f.at[pl.ds(0, 16 * (N - 1))])
    sent(11, rc_g.at[pl.ds(0, 8 * (N - 1))])
    arrived(12, out_ref.at[pl.ds(0, 2 * N - 1)])
    sent(12, out_ref.at[pl.ds(0, 2 * N - 1)])


def shards(query, new_keys, new_values, key_cache, value_cache, lengths, residual, out_weight,
           norm_gain, gate_weight, up_weight, down_weight):
    def vm(*shape, kind=F32):
        return pltpu.VMEM(shape, kind)

    hbm = pl.BlockSpec(memory_space=pltpu.HBM)
    pieces = pl.pallas_call(
        kernel,
        out_shape=jax.ShapeDtypeStruct((2 * N, 8, HD), BF16),
        in_specs=[hbm] * 12,
        out_specs=pl.BlockSpec(memory_space=pltpu.VMEM),
        scratch_shapes=[
            pltpu.SMEM((2,), jnp.int32),
            vm(2, 2, 4096, kind=BF16),
            vm(2, 2, 512, kind=BF16),
            vm(2, 2, 512, kind=BF16),
            vm(SPAN, 512, kind=BF16),
            vm(SPAN, 512, kind=BF16),
            vm(2, 32, 512, kind=BF16),
            vm(256, 512, kind=BF16),
            vm(512, kind=BF16),
            vm(512, 896, kind=BF16),
            vm(512, 896, kind=BF16),
            vm(896, 512, kind=BF16),
            vm(64, 512),
            vm(N, 4, HD),
            vm(2 * N, 512),
            vm(8 * N, HD),
            vm(8 * N, HD), vm(8 * N, HD),
            vm(4, HD), vm(N, 4, HD),
            vm(4, 8, 512, kind=BF16), vm(4, N, 8, 512, kind=BF16),
            vm(32 * N, HD), vm(32 * N, HD, kind=BF16), vm(32 * N, HD, kind=BF16),
            vm(16, HD, kind=BF16), vm(16 * N, HD, kind=BF16), vm(16 * N, HD),
            vm(8 * N, HD), vm(8 * N, HD),
            vm(8, HD, kind=BF16),
            pltpu.SemaphoreType.DMA((12,)),
            pltpu.SemaphoreType.DMA((13,)),
            pltpu.SemaphoreType.DMA((13,)),
            pltpu.SemaphoreType.REGULAR,
        ],
        compiler_params=pltpu.CompilerParams(
            collective_id=0, has_side_effects=True, vmem_limit_bytes=32 * 1024 * 1024
        ),
        name="layer",
    )(*[
        pltpu.with_memory_space_constraint(a, pltpu.HBM)
        for a in (lengths, query, new_keys, new_values, key_cache, value_cache, residual, out_weight,
                  norm_gain, gate_weight, up_weight, down_weight)
    ])
    pieces = pieces.reshape(2, N, 4, 2, HD)
    return pieces.transpose(3, 1, 0, 2, 4).reshape(2, 2 * N, 512)


def solution(mesh):
    in_specs = (
        P(None, "row", None),
        P(None, "row", None),
        P(None, "row", None),
        P("row", "col", None),
        P("row", "col", None),
        P("row"),
        P(None, None, "row"),
        P("col", "row"),
        P("row"),
        P("row", "col"),
        P("row", "col"),
        P("col", "row"),
    )
    out_specs = P(None, None, "row")
    return jax.shard_map(shards, mesh=mesh, in_specs=in_specs, out_specs=out_specs, check_vma=False)
```

```python
import functools
import math

import jax
import jax.numpy as jnp
from jax import lax
from jax.experimental import pallas as pl
from jax.experimental.pallas import tpu as pltpu
from jax.sharding import PartitionSpec as P

D = 8192
KV = 4
HD = 128
N = 16
SPAN = 384
VERY_LOW = -1e30
F32 = jnp.float32
BF16 = jnp.bfloat16
MESH = pl.DeviceIdType.MESH


def kernel(
    len_hbm, q_hbm, nk_hbm, nv_hbm, k_hbm, v_hbm, res_hbm, ow_hbm, gain_hbm, gw_hbm, uw_hbm, dw_hbm,
    out_ref,
    len_ref, q_v, nk_v, nv_v, k_v, v_v, res_v, ow_v, gain_v, gw_v, uw_v, dw_v,
    qbd, heads, res_s, mid_t,
    st_a, rc_a, st_b, rc_b, st_c, rc_c, st_e32, st_e, rc_e, st_f, rc_f, f32f, st_p, rc_p, kept, st_g, rc_g, both, order,
    load_sem, send_sem, recv_sem, met_sem,
):
    s = lax.axis_index("side")
    r = lax.axis_index("row")
    c = lax.axis_index("col")

    barrier = pltpu.get_barrier_semaphore()

    odd = lax.rem(c, 2)
    partner = c + 1 - 2 * odd

    def greet_row(i, _):
        pl.semaphore_signal(
            barrier,
            inc=1,
            device_id=(s, lax.rem(r + N // 2 + (i + 1) // 2 * (1 - 2 * lax.rem(i, 2)), N), c - odd + 1),
            device_id_type=MESH,
        )
        return 0

    def greet_col(i, _):
        pl.semaphore_signal(
            barrier, inc=1, device_id=(s, r, lax.rem(c + odd + 2 * i, N)), device_id_type=MESH
        )
        return 0

    def greet_side(i, _):
        pl.semaphore_signal(barrier, inc=1, device_id=(1 - s, r, 2 * i + 1), device_id_type=MESH)
        return 0

    lax.fori_loop(0, N - 1, greet_row, 0)

    @pl.when(odd == 1)
    def _():
        greet_col(0, 0)

    lax.fori_loop(1, N // 2, greet_col, 0)

    @pl.when(odd == 0)
    def _():
        pl.semaphore_signal(barrier, inc=1, device_id=(s, r, c + 1), device_id_type=MESH)

    lax.fori_loop(0, N // 2, greet_side, 0)

    loads = [
        pltpu.make_async_copy(src, dst, load_sem.at[i])
        for i, (src, dst) in enumerate(
            [
                (q_hbm, q_v),
                (k_hbm.at[s], k_v),
                (v_hbm.at[s], v_v),
                (nk_hbm, nk_v),
                (nv_hbm, nv_v),
                (res_hbm, res_v),
                (gain_hbm, gain_v),
                (ow_hbm, ow_v),
                (gw_hbm, gw_v),
                (uw_hbm, uw_v),
                (dw_hbm, dw_v),
                (len_hbm, len_ref),
            ]
        )
    ]
    for copy in loads:
        copy.start()

    def met_columns():
        @pl.when(odd == 0)
        def _():
            pl.semaphore_wait(barrier, N - 1)
            pl.semaphore_signal(met_sem, inc=1, device_id=(s, r, c + 1), device_id_type=MESH)

        @pl.when(odd == 1)
        def _():
            pl.semaphore_wait(met_sem, 1)

    def met_rows():
        @pl.when(odd == 1)
        def _():
            pl.semaphore_wait(barrier, 3 * N - 1)
            pl.semaphore_signal(met_sem, inc=1, device_id=(s, r, c - 1), device_id_type=MESH)

        @pl.when(odd == 0)
        def _():
            pl.semaphore_wait(met_sem, 1)

    def rows_at(ref, at, rows):
        return ref.at[pl.ds(pl.multiple_of(at * rows, rows), rows)]

    def offset(p):
        half = (p + 1) // 2
        return N + half * (2 * lax.rem(p, 2) - 1)

    def send(phase, source, target, device):
        pltpu.make_async_remote_copy(
            src_ref=source,
            dst_ref=target,
            send_sem=send_sem.at[phase],
            recv_sem=recv_sem.at[phase],
            device_id=device,
            device_id_type=MESH,
        ).start()

    def each(first, last, step):
        def one(i, _):
            step(i)
            return 0

        lax.fori_loop(first, last, one, 0)

    def to_columns(phase, source, target):
        def one(i):
            half = (i + 1) // 2
            peer = lax.rem(c + N // 2 + half * (1 - 2 * lax.rem(i, 2)), N)
            send(phase, source(peer), target, (s, r, peer))

        each(0, N - 1, one)

    def arrived(phase, ref):
        pltpu.make_async_copy(ref, ref, recv_sem.at[phase]).wait()

    def sent(phase, ref):
        pltpu.make_async_copy(ref, ref, send_sem.at[phase]).wait()

    qbd[...] = jnp.zeros_like(qbd)
    loads[0].wait()
    query = q_v[...].astype(F32)
    for t in range(2):
        mine = jnp.where(s == 0, query[t, 0:1, :], query[t, 1:2, :])
        for h in range(KV * 8):
            g = h // 8
            one_head = mine[:, h * HD : (h + 1) * HD]
            qbd[2 * h + t : 2 * h + t + 1, g * HD : (g + 1) * HD] = one_head
            heads[h // 2, 2 * (h % 2) + t : 2 * (h % 2) + t + 1, :] = one_head
    loads[1].wait()
    loads[11].wait()
    scale = 1.0 / math.sqrt(HD)
    scores = (
        lax.dot_general(
            qbd[...].astype(BF16), k_v[...], (((1,), (1,)), ((), ())), preferred_element_type=F32
        )
        * scale
    )
    live = c * SPAN + lax.broadcasted_iota(jnp.int32, scores.shape, 1) < len_ref[s]
    scores = jnp.where(live, scores, VERY_LOW)
    peak = jnp.max(scores, axis=1, keepdims=True)
    weights = jnp.where(live, jnp.exp(scores - peak), 0.0)
    total = jnp.sum(weights, axis=1, keepdims=True)
    loads[2].wait()
    summed = jnp.dot(weights.astype(BF16), v_v[...], preferred_element_type=F32)
    low_lane = lax.broadcasted_iota(jnp.int32, (64, HD), 1) < HD // 2
    stats = jnp.where(low_lane, peak, total)
    for o in range(N):
        g = o // 4
        st_a[8 * o : 8 * o + 4, :] = summed[4 * o : 4 * o + 4, g * HD : (g + 1) * HD]
        st_a[8 * o + 4 : 8 * o + 8, :] = stats[4 * o : 4 * o + 4, :]

    met_columns()
    to_columns(0, lambda peer: rows_at(st_a, peer, 8), rows_at(rc_a, c, 8))
    rows_at(rc_a, c, 8)[...] = rows_at(st_a, c, 8)[...]

    group_lanes = pl.ds(pl.multiple_of((c // 4) * HD, HD), HD)
    for copy in loads[3:8]:
        copy.wait()
    q4 = heads[c]
    fresh_k = nk_v[:, :, group_lanes].astype(F32)
    fresh_v = nv_v[:, :, group_lanes].astype(F32)
    nk = [jnp.where(s == 0, fresh_k[t, 0:1, :], fresh_k[t, 1:2, :]) for t in range(2)]
    nv = [jnp.where(s == 0, fresh_v[t, 0:1, :], fresh_v[t, 1:2, :]) for t in range(2)]
    second = lax.rem(lax.broadcasted_iota(jnp.int32, (4, HD), 0), 2) == 1
    f0 = jnp.broadcast_to(jnp.sum(q4 * nk[0], axis=1, keepdims=True) * scale, (4, HD))
    f1 = jnp.broadcast_to(jnp.sum(q4 * nk[1], axis=1, keepdims=True) * scale, (4, HD))
    f1 = jnp.where(second, f1, VERY_LOW)
    at = lax.broadcasted_iota(jnp.int32, (2 * N, 4 * N), 0)
    other = lax.rem(r + offset(at // 8 * 4 + lax.rem(at, 4)), N)
    wanted = lax.rem(at // 4, 2) * 2 * N + 2 * other + s
    chosen = lax.broadcasted_iota(jnp.int32, (2 * N, 4 * N), 1) == wanted
    res_s[...] = jnp.dot(
        jnp.where(chosen, 1.0, 0.0).astype(BF16), res_v[...].reshape(4 * N, 512), preferred_element_type=F32
    )
    gains = gain_v[...].astype(F32).reshape(1, 512)

    arrived(0, rc_a.at[pl.ds(0, 8 * (N - 1))])
    blocks = rc_a[...].reshape(N, 8, HD)
    sums, stat = blocks[:, 0:4, :], blocks[:, 4:8, :]
    low = lax.broadcasted_iota(jnp.int32, (N, 4, HD), 2) < HD // 2
    turned = pltpu.roll(stat, HD // 2, 2)
    peaks = jnp.where(low, stat, turned)
    totals = jnp.where(low, turned, stat)
    top = jnp.maximum(jnp.max(peaks, axis=0), jnp.maximum(f0, f1))
    share = jnp.exp(peaks - top[None])
    e0 = jnp.exp(f0 - top)
    e1 = jnp.where(second, jnp.exp(f1 - top), 0.0)
    whole = jnp.sum(share * totals, axis=0) + e0 + e1
    mixed = jnp.sum(share * sums, axis=0) + e0 * nv[0] + e1 * nv[1]
    st_b[...] = (mixed / whole).astype(BF16).astype(F32)

    met_rows()
    def give_attended(k):
        def one(i):
            p = 4 * k + 3 - i
            send(1 + k, st_b, rc_b.at[p], (s, lax.rem(r + 2 * N - offset(p), N), c))

        each(0, 4 if k else 3, one)

    for k in range(3, -1, -1):
        give_attended(k)
    rc_b[0] = st_b[...]

    def project(k):
        attended = jnp.concatenate(
            [
                jnp.concatenate([rc_b[4 * k : 4 * k + 4, 2 * j + t, :] for j in range(2)], axis=1)
                for t in range(2)
            ],
            axis=0,
        )
        st_c[k] = jnp.dot(attended.astype(BF16), ow_v[...], preferred_element_type=F32).astype(BF16)
        to_columns(5 + k, lambda peer: st_c.at[k], rc_c.at[k, c])
        rc_c[k, c] = st_c[k]

    def scatter(ref, value, count, stride, base):
        for t in range(2):
            for m in range(count):
                ref[pl.ds(base + 2 * m + t, 4, stride=stride), :] = value[
                    4 * t : 4 * (t + 1), m * HD : (m + 1) * HD
                ]

    def lift(k):
        mid = res_s[8 * k : 8 * (k + 1), :] + jnp.sum(rc_c[k].astype(F32), axis=0)
        lifted = (mid * gains).astype(BF16)
        squares = jnp.broadcast_to(jnp.sum(mid * mid, axis=1, keepdims=True), (8, HD))
        high = squares.astype(BF16).astype(F32)
        base = 128 * k
        scatter(st_e32, high, 1, 32, base + 14)
        scatter(st_e32, squares - high, 1, 32, base + 30)
        if k == 0:
            loads[8].wait()
        scatter(st_e32, jnp.dot(lifted, gw_v[...], preferred_element_type=F32), 7, 32, base)
        if k == 0:
            loads[9].wait()
        scatter(st_e32, jnp.dot(lifted, uw_v[...], preferred_element_type=F32), 7, 32, base + 16)
        st_e[base : base + 128, :] = st_e32[base : base + 128, :].astype(BF16)

        def one(p):
            owner = lax.rem(r + N // 2 + offset(p), N)
            send(9, rows_at(st_e, p, 32), rows_at(rc_e, p, 32), (s, owner, c))

        each(4 * k, 4 * k + (4 if k < 3 else 3), one)
        half = own_half(mid)
        at = 4 * s + 3 - k
        for t in range(2):
            for i in range(4):
                mid_t[at, 4 * t + 3 - i : 4 * t + 4 - i, :] = half[4 * t + i : 4 * t + i + 1, :]
        send(22, mid_t.at[at], mid_t.at[at], (1 - s, r, c))

    def own_half(value):
        return jnp.where(odd == 0, value[:, :256], value[:, 256:])

    arrived(1, rc_b.at[pl.ds(0, 3)])
    project(0)
    arrived(2, rc_b.at[pl.ds(0, 4)])
    project(1)
    arrived(3, rc_b.at[pl.ds(0, 4)])
    project(2)
    arrived(4, rc_b.at[pl.ds(0, 4)])
    project(3)
    arrived(5, rc_c.at[0, pl.ds(0, N - 1)])
    lift(0)
    arrived(6, rc_c.at[1, pl.ds(0, N - 1)])
    lift(1)
    arrived(7, rc_c.at[2, pl.ds(0, N - 1)])
    lift(2)
    arrived(8, rc_c.at[3, pl.ds(0, N - 1)])
    lift(3)
    rc_e[32 * (N - 1) :, :] = st_e[32 * (N - 1) :, :]
    arrived(9, rc_e.at[pl.ds(0, 32 * (N - 1))])
    lifts = jnp.sum(rc_e[...].astype(F32).reshape(N, 32, HD), axis=0)
    gate, up = lifts[0:16], lifts[16:32]
    inv0 = lax.rsqrt((gate[14:15] + up[14:15]) / D + 1e-05)
    inv1 = lax.rsqrt((gate[15:16] + up[15:16]) / D + 1e-05)
    inv = jnp.where(lax.rem(lax.broadcasted_iota(jnp.int32, (16, HD), 0), 2) == 1, inv1, inv0)
    gate, up = gate * inv, up * inv
    st_f[...] = (gate / (1.0 + jnp.exp(-gate)) * up).astype(BF16)

    def give_act(k):
        def one(i):
            p = 4 * k + 3 - i
            send(10 + k, st_f, rows_at(rc_f, p, 16), (s, lax.rem(r + 2 * N - offset(p), N), c))

        each(0, 4 if k else 3, one)

    for k in range(3, -1, -1):
        give_act(k)
    rc_f[0:16, :] = st_f[...]
    target = lax.broadcasted_iota(jnp.int32, (4 * N, 4 * N), 0)
    source = lax.broadcasted_iota(jnp.int32, (4 * N, 4 * N), 1)
    row = lax.rem(r + N // 2 + offset(source // 16 * 4 + lax.rem(source, 4)), N)
    lands = lax.rem(source // 4, 2) * 2 * N + 2 * row + lax.rem(source // 8, 2)
    order[...] = jnp.where(target == lands, 1.0, 0.0).astype(BF16)
    loads[10].wait()

    def down(k):
        f32f[64 * k : 64 * (k + 1), :] = rc_f[64 * k : 64 * (k + 1), :].astype(F32)
        act = jnp.concatenate(
            [
                jnp.concatenate(
                    [f32f[pl.ds(64 * k + 2 * m + t, 4, stride=16), :] for m in range(7)], axis=1
                )
                for t in range(2)
            ],
            axis=0,
        )
        part = jnp.dot(act.astype(BF16), dw_v[...], preferred_element_type=F32)
        st_p[k] = jnp.where(odd == 0, part[:, 256:], part[:, :256])
        send(14 + k, st_p.at[k], rc_p.at[k], (s, r, partner))
        kept[k] = own_half(part)

    spot = s * (N // 2) + c // 2

    def merge(k):
        st_g[k] = (kept[k] + rc_p[k]).astype(BF16)

        def one(i):
            other = lax.rem(spot + i, N)
            peer = (other // (N // 2), r, 2 * lax.rem(other, N // 2) + odd)
            send(18 + k, st_g.at[k], rc_g.at[k, spot], peer)

        each(1, N, one)
        rc_g[k, spot] = st_g[k]

    def finish(k):
        for side in range(2):
            parts = jnp.sum(rc_g[k, 8 * side : 8 * side + 8].astype(F32), axis=0)
            both[odd, k, side] = (mid_t[4 * side + k] + parts).astype(BF16)
        send(23, both.at[odd, k], both.at[odd, k], (s, r, partner))

    arrived(10, rc_f.at[pl.ds(0, 48)])
    down(0)
    arrived(11, rc_f.at[pl.ds(0, 64)])
    down(1)
    arrived(14, rc_p.at[0])
    merge(0)
    arrived(12, rc_f.at[pl.ds(0, 64)])
    down(2)
    arrived(15, rc_p.at[1])
    merge(1)
    arrived(13, rc_f.at[pl.ds(0, 64)])
    down(3)
    arrived(16, rc_p.at[2])
    merge(2)
    arrived(17, rc_p.at[3])
    merge(3)
    arrived(22, mid_t.at[pl.ds(0, 4)])
    arrived(18, rc_g.at[0, pl.ds(0, N - 1)])
    finish(0)
    arrived(19, rc_g.at[1, pl.ds(0, N - 1)])
    finish(1)
    arrived(20, rc_g.at[2, pl.ds(0, N - 1)])
    finish(2)
    arrived(21, rc_g.at[3, pl.ds(0, N - 1)])
    finish(3)
    arrived(23, both.at[0])
    rows = jnp.concatenate([both[h].astype(F32).reshape(4 * N, 256) for h in range(2)], axis=1)
    result = jnp.dot(order[...], rows.astype(BF16), preferred_element_type=F32)
    out_ref[...] = result.astype(BF16).reshape(2, 2 * N, 512)

    sent(0, rc_a.at[pl.ds(0, 8 * (N - 1))])
    sent(1, rc_b.at[pl.ds(0, 3)])
    sent(2, rc_b.at[pl.ds(0, 4)])
    sent(3, rc_b.at[pl.ds(0, 4)])
    sent(4, rc_b.at[pl.ds(0, 4)])
    sent(5, rc_c.at[0, pl.ds(0, N - 1)])
    sent(6, rc_c.at[1, pl.ds(0, N - 1)])
    sent(7, rc_c.at[2, pl.ds(0, N - 1)])
    sent(8, rc_c.at[3, pl.ds(0, N - 1)])
    sent(9, rc_e.at[pl.ds(0, 32 * (N - 1))])
    sent(10, rc_f.at[pl.ds(0, 48)])
    sent(11, rc_f.at[pl.ds(0, 64)])
    sent(12, rc_f.at[pl.ds(0, 64)])
    sent(13, rc_f.at[pl.ds(0, 64)])
    sent(14, rc_p.at[0])
    sent(15, rc_p.at[1])
    sent(16, rc_p.at[2])
    sent(17, rc_p.at[3])
    sent(18, rc_g.at[0, pl.ds(0, N - 1)])
    sent(19, rc_g.at[1, pl.ds(0, N - 1)])
    sent(20, rc_g.at[2, pl.ds(0, N - 1)])
    sent(21, rc_g.at[3, pl.ds(0, N - 1)])
    sent(22, mid_t.at[pl.ds(0, 4)])
    sent(23, both.at[0])


def shards(query, new_keys, new_values, key_cache, value_cache, lengths, residual, out_weight,
           norm_gain, gate_weight, up_weight, down_weight):
    def vm(*shape, kind=F32):
        return pltpu.VMEM(shape, kind)

    hbm = pl.BlockSpec(memory_space=pltpu.HBM)
    return pl.pallas_call(
        kernel,
        out_shape=jax.ShapeDtypeStruct((2, 2 * N, 512), BF16),
        in_specs=[hbm] * 12,
        out_specs=pl.BlockSpec(memory_space=pltpu.VMEM),
        scratch_shapes=[
            pltpu.SMEM((2,), jnp.int32),
            vm(2, 2, 4096, kind=BF16),
            vm(2, 2, 512, kind=BF16),
            vm(2, 2, 512, kind=BF16),
            vm(SPAN, 512, kind=BF16),
            vm(SPAN, 512, kind=BF16),
            vm(2, 32, 512, kind=BF16),
            vm(256, 512, kind=BF16),
            vm(512, kind=BF16),
            vm(512, 896, kind=BF16),
            vm(512, 896, kind=BF16),
            vm(896, 512, kind=BF16),
            vm(64, 512),
            vm(N, 4, HD),
            vm(2 * N, 512),
            vm(8, 8, 256),
            vm(8 * N, HD), vm(8 * N, HD),
            vm(4, HD), vm(N, 4, HD),
            vm(4, 8, 512, kind=BF16), vm(4, N, 8, 512, kind=BF16),
            vm(32 * N, HD), vm(32 * N, HD, kind=BF16), vm(32 * N, HD, kind=BF16),
            vm(16, HD, kind=BF16), vm(16 * N, HD, kind=BF16), vm(16 * N, HD),
            vm(4, 8, 256), vm(4, 8, 256), vm(4, 8, 256),
            vm(4, 8, 256, kind=BF16), vm(4, N, 8, 256, kind=BF16),
            vm(2, 4, 2, 8, 256, kind=BF16),
            vm(4 * N, 4 * N, kind=BF16),
            pltpu.SemaphoreType.DMA((12,)),
            pltpu.SemaphoreType.DMA((24,)),
            pltpu.SemaphoreType.DMA((24,)),
            pltpu.SemaphoreType.REGULAR,
        ],
        compiler_params=pltpu.CompilerParams(
            collective_id=0, has_side_effects=True, vmem_limit_bytes=32 * 1024 * 1024
        ),
        name="layer",
    )(*[
        pltpu.with_memory_space_constraint(a, pltpu.HBM)
        for a in (lengths, query, new_keys, new_values, key_cache, value_cache, residual, out_weight,
                  norm_gain, gate_weight, up_weight, down_weight)
    ])


def solution(mesh):
    in_specs = (
        P(None, "row", None),
        P(None, "row", None),
        P(None, "row", None),
        P("row", "col", None),
        P("row", "col", None),
        P("row"),
        P(None, None, "row"),
        P("col", "row"),
        P("row"),
        P("row", "col"),
        P("row", "col"),
        P("col", "row"),
    )
    out_specs = P(None, None, "row")
    return jax.shard_map(shards, mesh=mesh, in_specs=in_specs, out_specs=out_specs, check_vma=False)
```

```python
import functools
import math

import jax
import jax.numpy as jnp
from jax import lax
from jax.experimental import pallas as pl
from jax.experimental.pallas import tpu as pltpu
from jax.sharding import PartitionSpec as P

D = 8192
KV = 4
HD = 128
N = 16
SPAN = 384
VERY_LOW = -1e30
F32 = jnp.float32
BF16 = jnp.bfloat16
MESH = pl.DeviceIdType.MESH


def kernel(
    len_hbm, q_hbm, nk_hbm, nv_hbm, k_hbm, v_hbm, res_hbm, ow_hbm, gain_hbm, gw_hbm, uw_hbm, dw_hbm,
    out_ref,
    len_ref, q_v, nk_v, nv_v, k_v, v_v, res_v, ow_v, gain_v, gw_v, uw_v, dw_v,
    qbd, heads, res_s, mid_t,
    st_a32, st_a, rc_a, st_b, rc_b, st_c, rc_c, st_e32, st_e, rc_e, st_f, rc_f, f32f, st_g, rc_g, st_x, rc_x, both, order,
    load_sem, send_sem, recv_sem, met_sem,
):
    s = lax.axis_index("side")
    r = lax.axis_index("row")
    c = lax.axis_index("col")

    barrier = pltpu.get_barrier_semaphore()

    odd = lax.rem(c, 2)
    plane = c // 8
    lane = lax.rem(c, 8)
    across = 2 * s + plane

    def greet_row(i, _):
        pl.semaphore_signal(
            barrier,
            inc=1,
            device_id=(s, lax.rem(r + N // 2 + (i + 1) // 2 * (1 - 2 * lax.rem(i, 2)), N), c - odd + 1),
            device_id_type=MESH,
        )
        return 0

    def greet_col(i, _):
        pl.semaphore_signal(
            barrier, inc=1, device_id=(s, r, lax.rem(c + odd + 2 * i, N)), device_id_type=MESH
        )
        return 0

    def greet_side(i, _):
        pl.semaphore_signal(barrier, inc=1, device_id=(1 - s, r, 2 * i + 1), device_id_type=MESH)
        return 0

    lax.fori_loop(0, N - 1, greet_row, 0)

    @pl.when(odd == 1)
    def _():
        greet_col(0, 0)

    lax.fori_loop(1, N // 2, greet_col, 0)

    @pl.when(odd == 0)
    def _():
        pl.semaphore_signal(barrier, inc=1, device_id=(s, r, c + 1), device_id_type=MESH)

    lax.fori_loop(0, N // 2, greet_side, 0)

    loads = [
        pltpu.make_async_copy(src, dst, load_sem.at[i])
        for i, (src, dst) in enumerate(
            [
                (q_hbm, q_v),
                (k_hbm.at[s], k_v),
                (v_hbm.at[s], v_v),
                (nk_hbm, nk_v),
                (nv_hbm, nv_v),
                (res_hbm, res_v),
                (gain_hbm, gain_v),
                (ow_hbm, ow_v),
                (gw_hbm, gw_v),
                (uw_hbm, uw_v),
                (dw_hbm, dw_v),
                (len_hbm, len_ref),
            ]
        )
    ]
    for copy in loads:
        copy.start()

    def met_columns():
        @pl.when(odd == 0)
        def _():
            pl.semaphore_wait(barrier, N - 1)
            pl.semaphore_signal(met_sem, inc=1, device_id=(s, r, c + 1), device_id_type=MESH)

        @pl.when(odd == 1)
        def _():
            pl.semaphore_wait(met_sem, 1)

    def met_rows():
        @pl.when(odd == 1)
        def _():
            pl.semaphore_wait(barrier, 3 * N - 1)
            pl.semaphore_signal(met_sem, inc=1, device_id=(s, r, c - 1), device_id_type=MESH)

        @pl.when(odd == 0)
        def _():
            pl.semaphore_wait(met_sem, 1)

    def rows_at(ref, at, rows):
        return ref.at[pl.ds(pl.multiple_of(at * rows, rows), rows)]

    def offset(p):
        half = (p + 1) // 2
        return N + half * (2 * lax.rem(p, 2) - 1)

    def send(phase, source, target, device):
        pltpu.make_async_remote_copy(
            src_ref=source,
            dst_ref=target,
            send_sem=send_sem.at[phase],
            recv_sem=recv_sem.at[phase],
            device_id=device,
            device_id_type=MESH,
        ).start()

    def each(first, last, step):
        def one(i, _):
            step(i)
            return 0

        lax.fori_loop(first, last, one, 0)

    def to_columns(phase, source, target):
        def one(i):
            half = (i + 1) // 2
            peer = lax.rem(c + N // 2 + half * (1 - 2 * lax.rem(i, 2)), N)
            send(phase, source(peer), target, (s, r, peer))

        each(0, N - 1, one)

    def arrived(phase, ref):
        pltpu.make_async_copy(ref, ref, recv_sem.at[phase]).wait()

    def sent(phase, ref):
        pltpu.make_async_copy(ref, ref, send_sem.at[phase]).wait()

    qbd[...] = jnp.zeros_like(qbd)
    loads[0].wait()
    query = q_v[...].astype(F32)
    for t in range(2):
        mine = jnp.where(s == 0, query[t, 0:1, :], query[t, 1:2, :])
        for h in range(KV * 8):
            g = h // 8
            one_head = mine[:, h * HD : (h + 1) * HD]
            qbd[2 * h + t : 2 * h + t + 1, g * HD : (g + 1) * HD] = one_head
            heads[h // 2, 2 * (h % 2) + t : 2 * (h % 2) + t + 1, :] = one_head
    loads[1].wait()
    loads[11].wait()
    scale = 1.0 / math.sqrt(HD)
    scores = (
        lax.dot_general(
            qbd[...].astype(BF16), k_v[...], (((1,), (1,)), ((), ())), preferred_element_type=F32
        )
        * scale
    )
    live = c * SPAN + lax.broadcasted_iota(jnp.int32, scores.shape, 1) < len_ref[s]
    scores = jnp.where(live, scores, VERY_LOW)
    peak = jnp.max(scores, axis=1, keepdims=True).astype(BF16).astype(F32)
    weights = jnp.where(live, jnp.exp(scores - peak), 0.0)
    total = jnp.sum(weights, axis=1, keepdims=True)
    loads[2].wait()
    summed = jnp.dot(weights.astype(BF16), v_v[...], preferred_element_type=F32)
    low_lane = lax.broadcasted_iota(jnp.int32, (64, HD), 1) < HD // 2
    stats = jnp.where(low_lane, peak, total)
    for o in range(N):
        g = o // 4
        st_a32[8 * o : 8 * o + 4, :] = summed[4 * o : 4 * o + 4, g * HD : (g + 1) * HD]
        st_a32[8 * o + 4 : 8 * o + 8, :] = stats[4 * o : 4 * o + 4, :]

    st_a[...] = st_a32[...].reshape(N, 8, HD).astype(BF16)
    met_columns()
    to_columns(0, lambda peer: st_a.at[peer], rc_a.at[c])
    rc_a[c] = st_a[c]

    group_lanes = pl.ds(pl.multiple_of((c // 4) * HD, HD), HD)
    for copy in loads[3:8]:
        copy.wait()
    q4 = heads[c]
    fresh_k = nk_v[:, :, group_lanes].astype(F32)
    fresh_v = nv_v[:, :, group_lanes].astype(F32)
    nk = [jnp.where(s == 0, fresh_k[t, 0:1, :], fresh_k[t, 1:2, :]) for t in range(2)]
    nv = [jnp.where(s == 0, fresh_v[t, 0:1, :], fresh_v[t, 1:2, :]) for t in range(2)]
    second = lax.rem(lax.broadcasted_iota(jnp.int32, (4, HD), 0), 2) == 1
    f0 = jnp.broadcast_to(jnp.sum(q4 * nk[0], axis=1, keepdims=True) * scale, (4, HD))
    f1 = jnp.broadcast_to(jnp.sum(q4 * nk[1], axis=1, keepdims=True) * scale, (4, HD))
    f1 = jnp.where(second, f1, VERY_LOW)
    at = lax.broadcasted_iota(jnp.int32, (2 * N, 4 * N), 0)
    other = lax.rem(r + offset(at // 8 * 4 + lax.rem(at, 4)), N)
    wanted = lax.rem(at // 4, 2) * 2 * N + 2 * other + s
    chosen = lax.broadcasted_iota(jnp.int32, (2 * N, 4 * N), 1) == wanted
    res_s[...] = jnp.dot(
        jnp.where(chosen, 1.0, 0.0).astype(BF16), res_v[...].reshape(4 * N, 512), preferred_element_type=F32
    )
    gains = gain_v[...].astype(F32).reshape(1, 512)

    arrived(0, rc_a.at[pl.ds(0, N - 1)])
    blocks = rc_a[...].astype(F32)
    sums, stat = blocks[:, 0:4, :], blocks[:, 4:8, :]
    low = lax.broadcasted_iota(jnp.int32, (N, 4, HD), 2) < HD // 2
    turned = pltpu.roll(stat, HD // 2, 2)
    peaks = jnp.where(low, stat, turned)
    totals = jnp.where(low, turned, stat)
    top = jnp.maximum(jnp.max(peaks, axis=0), jnp.maximum(f0, f1))
    share = jnp.exp(peaks - top[None])
    e0 = jnp.exp(f0 - top)
    e1 = jnp.where(second, jnp.exp(f1 - top), 0.0)
    whole = jnp.sum(share * totals, axis=0) + e0 + e1
    mixed = jnp.sum(share * sums, axis=0) + e0 * nv[0] + e1 * nv[1]
    st_b[...] = (mixed / whole).astype(BF16).astype(F32)

    met_rows()
    def give_attended(k):
        def one(i):
            p = 4 * k + 3 - i
            send(1 + k, st_b, rc_b.at[p], (s, lax.rem(r + 2 * N - offset(p), N), c))

        each(0, 4 if k else 3, one)

    for k in range(3, -1, -1):
        give_attended(k)
    rc_b[0] = st_b[...]

    def project(k):
        attended = jnp.concatenate(
            [
                jnp.concatenate([rc_b[4 * k : 4 * k + 4, 2 * j + t, :] for j in range(2)], axis=1)
                for t in range(2)
            ],
            axis=0,
        )
        st_c[k] = jnp.dot(attended.astype(BF16), ow_v[...], preferred_element_type=F32).astype(BF16)
        to_columns(5 + k, lambda peer: st_c.at[k], rc_c.at[k, c])
        rc_c[k, c] = st_c[k]

    def scatter(ref, value, count, stride, base):
        for t in range(2):
            for m in range(count):
                ref[pl.ds(base + 2 * m + t, 4, stride=stride), :] = value[
                    4 * t : 4 * (t + 1), m * HD : (m + 1) * HD
                ]

    def lift(k):
        mid = res_s[8 * k : 8 * (k + 1), :] + jnp.sum(rc_c[k].astype(F32), axis=0)
        lifted = (mid * gains).astype(BF16)
        squares = jnp.broadcast_to(jnp.sum(mid * mid, axis=1, keepdims=True), (8, HD))
        high = squares.astype(BF16).astype(F32)
        base = 128 * k
        scatter(st_e32, high, 1, 32, base + 14)
        scatter(st_e32, squares - high, 1, 32, base + 30)
        if k == 0:
            loads[8].wait()
        scatter(st_e32, jnp.dot(lifted, gw_v[...], preferred_element_type=F32), 7, 32, base)
        if k == 0:
            loads[9].wait()
        scatter(st_e32, jnp.dot(lifted, uw_v[...], preferred_element_type=F32), 7, 32, base + 16)
        st_e[base : base + 128, :] = st_e32[base : base + 128, :].astype(BF16)

        def one(p):
            owner = lax.rem(r + N // 2 + offset(p), N)
            send(9, rows_at(st_e, p, 32), rows_at(rc_e, p, 32), (s, owner, c))

        each(4 * k, 4 * k + (4 if k < 3 else 3), one)
        at = 4 * s + 3 - k
        for t in range(2):
            for i in range(4):
                mid_t[at, 4 * t + 3 - i : 4 * t + 4 - i, :] = mid[4 * t + i : 4 * t + i + 1, :]
        send(22, mid_t.at[at], mid_t.at[at], (1 - s, r, c))

    arrived(1, rc_b.at[pl.ds(0, 3)])
    project(0)
    arrived(2, rc_b.at[pl.ds(0, 4)])
    project(1)
    arrived(3, rc_b.at[pl.ds(0, 4)])
    project(2)
    arrived(4, rc_b.at[pl.ds(0, 4)])
    project(3)
    arrived(5, rc_c.at[0, pl.ds(0, N - 1)])
    lift(0)
    arrived(6, rc_c.at[1, pl.ds(0, N - 1)])
    lift(1)
    arrived(7, rc_c.at[2, pl.ds(0, N - 1)])
    lift(2)
    arrived(8, rc_c.at[3, pl.ds(0, N - 1)])
    lift(3)
    rc_e[32 * (N - 1) :, :] = st_e[32 * (N - 1) :, :]
    arrived(9, rc_e.at[pl.ds(0, 32 * (N - 1))])
    lifts = jnp.sum(rc_e[...].astype(F32).reshape(N, 32, HD), axis=0)
    gate, up = lifts[0:16], lifts[16:32]
    inv0 = lax.rsqrt((gate[14:15] + up[14:15]) / D + 1e-05)
    inv1 = lax.rsqrt((gate[15:16] + up[15:16]) / D + 1e-05)
    inv = jnp.where(lax.rem(lax.broadcasted_iota(jnp.int32, (16, HD), 0), 2) == 1, inv1, inv0)
    gate, up = gate * inv, up * inv
    st_f[...] = (gate / (1.0 + jnp.exp(-gate)) * up).astype(BF16)

    def give_act(k):
        def one(i):
            p = 4 * k + 3 - i
            send(10 + k, st_f, rows_at(rc_f, p, 16), (s, lax.rem(r + 2 * N - offset(p), N), c))

        each(0, 4 if k else 3, one)

    for k in range(3, -1, -1):
        give_act(k)
    rc_f[0:16, :] = st_f[...]
    target = lax.broadcasted_iota(jnp.int32, (4 * N, 4 * N), 0)
    source = lax.broadcasted_iota(jnp.int32, (4 * N, 4 * N), 1)
    row = lax.rem(r + N // 2 + offset(source // 16 * 4 + lax.rem(source, 4)), N)
    lands = lax.rem(source // 4, 2) * 2 * N + 2 * row + lax.rem(source // 8, 2)
    order[...] = jnp.where(target == lands, 1.0, 0.0).astype(BF16)
    loads[10].wait()

    def down(k):
        f32f[64 * k : 64 * (k + 1), :] = rc_f[64 * k : 64 * (k + 1), :].astype(F32)
        act = jnp.concatenate(
            [
                jnp.concatenate(
                    [f32f[pl.ds(64 * k + 2 * m + t, 4, stride=16), :] for m in range(7)], axis=1
                )
                for t in range(2)
            ],
            axis=0,
        )
        part = jnp.dot(act.astype(BF16), dw_v[...], preferred_element_type=F32)
        st_g[k] = part.astype(BF16)

        def one(i):
            send(14 + k, st_g.at[k], rc_g.at[k, lane], (s, r, 8 * plane + lax.rem(lane + i, 8)))

        each(1, 8, one)
        rc_g[k, lane] = st_g[k]

    def hand_on(k):
        st_x[k] = jnp.sum(rc_g[k].astype(F32), axis=0).astype(BF16)
        for i in (2, 1, 3):
            other = lax.rem(across + i, 4)
            send(18 + k, st_x.at[k], rc_x.at[k, across], (other // 2, r, 8 * lax.rem(other, 2) + lane))
        rc_x[k, across] = st_x[k]

    def finish(k):
        for side in range(2):
            parts = rc_x[k, 2 * side].astype(F32) + rc_x[k, 2 * side + 1].astype(F32)
            both[k, side] = (mid_t[4 * side + k] + parts).astype(BF16)

    arrived(10, rc_f.at[pl.ds(0, 48)])
    down(0)
    arrived(11, rc_f.at[pl.ds(0, 64)])
    down(1)
    arrived(12, rc_f.at[pl.ds(0, 64)])
    down(2)
    arrived(13, rc_f.at[pl.ds(0, 64)])
    down(3)
    arrived(14, rc_g.at[0, pl.ds(0, 7)])
    hand_on(0)
    arrived(15, rc_g.at[1, pl.ds(0, 7)])
    hand_on(1)
    arrived(16, rc_g.at[2, pl.ds(0, 7)])
    hand_on(2)
    arrived(17, rc_g.at[3, pl.ds(0, 7)])
    hand_on(3)
    arrived(22, mid_t.at[pl.ds(0, 4)])
    arrived(18, rc_x.at[0, pl.ds(0, 3)])
    finish(0)
    arrived(19, rc_x.at[1, pl.ds(0, 3)])
    finish(1)
    arrived(20, rc_x.at[2, pl.ds(0, 3)])
    finish(2)
    arrived(21, rc_x.at[3, pl.ds(0, 3)])
    finish(3)
    rows = both[...].astype(F32).reshape(4 * N, 512).astype(BF16)
    result = jnp.dot(order[...], rows, preferred_element_type=F32)
    out_ref[...] = result.astype(BF16).reshape(2, 2 * N, 512)

    sent(0, rc_a.at[pl.ds(0, N - 1)])
    sent(1, rc_b.at[pl.ds(0, 3)])
    sent(2, rc_b.at[pl.ds(0, 4)])
    sent(3, rc_b.at[pl.ds(0, 4)])
    sent(4, rc_b.at[pl.ds(0, 4)])
    sent(5, rc_c.at[0, pl.ds(0, N - 1)])
    sent(6, rc_c.at[1, pl.ds(0, N - 1)])
    sent(7, rc_c.at[2, pl.ds(0, N - 1)])
    sent(8, rc_c.at[3, pl.ds(0, N - 1)])
    sent(9, rc_e.at[pl.ds(0, 32 * (N - 1))])
    sent(10, rc_f.at[pl.ds(0, 48)])
    sent(11, rc_f.at[pl.ds(0, 64)])
    sent(12, rc_f.at[pl.ds(0, 64)])
    sent(13, rc_f.at[pl.ds(0, 64)])
    sent(14, rc_g.at[0, pl.ds(0, 7)])
    sent(15, rc_g.at[1, pl.ds(0, 7)])
    sent(16, rc_g.at[2, pl.ds(0, 7)])
    sent(17, rc_g.at[3, pl.ds(0, 7)])
    sent(18, rc_x.at[0, pl.ds(0, 3)])
    sent(19, rc_x.at[1, pl.ds(0, 3)])
    sent(20, rc_x.at[2, pl.ds(0, 3)])
    sent(21, rc_x.at[3, pl.ds(0, 3)])
    sent(22, mid_t.at[pl.ds(0, 4)])


def shards(query, new_keys, new_values, key_cache, value_cache, lengths, residual, out_weight,
           norm_gain, gate_weight, up_weight, down_weight):
    def vm(*shape, kind=F32):
        return pltpu.VMEM(shape, kind)

    hbm = pl.BlockSpec(memory_space=pltpu.HBM)
    return pl.pallas_call(
        kernel,
        out_shape=jax.ShapeDtypeStruct((2, 2 * N, 512), BF16),
        in_specs=[hbm] * 12,
        out_specs=pl.BlockSpec(memory_space=pltpu.VMEM),
        scratch_shapes=[
            pltpu.SMEM((2,), jnp.int32),
            vm(2, 2, 4096, kind=BF16),
            vm(2, 2, 512, kind=BF16),
            vm(2, 2, 512, kind=BF16),
            vm(SPAN, 512, kind=BF16),
            vm(SPAN, 512, kind=BF16),
            vm(2, 32, 512, kind=BF16),
            vm(256, 512, kind=BF16),
            vm(512, kind=BF16),
            vm(512, 896, kind=BF16),
            vm(512, 896, kind=BF16),
            vm(896, 512, kind=BF16),
            vm(64, 512),
            vm(N, 4, HD),
            vm(2 * N, 512),
            vm(8, 8, 512),
            vm(8 * N, HD), vm(N, 8, HD, kind=BF16), vm(N, 8, HD, kind=BF16),
            vm(4, HD), vm(N, 4, HD),
            vm(4, 8, 512, kind=BF16), vm(4, N, 8, 512, kind=BF16),
            vm(32 * N, HD), vm(32 * N, HD, kind=BF16), vm(32 * N, HD, kind=BF16),
            vm(16, HD, kind=BF16), vm(16 * N, HD, kind=BF16), vm(16 * N, HD),
            vm(4, 8, 512, kind=BF16), vm(4, 8, 8, 512, kind=BF16),
            vm(4, 8, 512, kind=BF16), vm(4, 4, 8, 512, kind=BF16),
            vm(4, 2, 8, 512, kind=BF16),
            vm(4 * N, 4 * N, kind=BF16),
            pltpu.SemaphoreType.DMA((12,)),
            pltpu.SemaphoreType.DMA((23,)),
            pltpu.SemaphoreType.DMA((23,)),
            pltpu.SemaphoreType.REGULAR,
        ],
        compiler_params=pltpu.CompilerParams(
            collective_id=0, has_side_effects=True, vmem_limit_bytes=32 * 1024 * 1024
        ),
        name="layer",
    )(*[
        pltpu.with_memory_space_constraint(a, pltpu.HBM)
        for a in (lengths, query, new_keys, new_values, key_cache, value_cache, residual, out_weight,
                  norm_gain, gate_weight, up_weight, down_weight)
    ])


def solution(mesh):
    in_specs = (
        P(None, "row", None),
        P(None, "row", None),
        P(None, "row", None),
        P("row", "col", None),
        P("row", "col", None),
        P("row"),
        P(None, None, "row"),
        P("col", "row"),
        P("row"),
        P("row", "col"),
        P("row", "col"),
        P("col", "row"),
    )
    out_specs = P(None, None, "row")
    return jax.shard_map(shards, mesh=mesh, in_specs=in_specs, out_specs=out_specs, check_vma=False)
```

```python
import functools
import math

import jax
import jax.numpy as jnp
from jax import lax
from jax.experimental import pallas as pl
from jax.experimental.pallas import tpu as pltpu
from jax.sharding import PartitionSpec as P

D = 8192
KV = 4
HD = 128
N = 16
SPAN = 384
VERY_LOW = -1e30
F32 = jnp.float32
BF16 = jnp.bfloat16
MESH = pl.DeviceIdType.MESH


def kernel(
    len_hbm, q_hbm, nk_hbm, nv_hbm, k_hbm, v_hbm, res_hbm, ow_hbm, gain_hbm, gw_hbm, uw_hbm, dw_hbm,
    out_ref,
    len_ref, q_v, nk_v, nv_v, k_v, v_v, res_v, ow_v, gain_v, gw_v, uw_v, dw_v,
    qbd, heads, res_s, mid_t,
    st_a32, st_a, rc_a, st_b, rc_b, st_c, rc_c, st_e32, st_e, rc_e, st_f, rc_f, f32f, st_g, rc_g, st_x, rc_x, both, order,
    load_sem, send_sem, recv_sem, met_sem,
):
    s = lax.axis_index("side")
    r = lax.axis_index("row")
    c = lax.axis_index("col")

    barrier = pltpu.get_barrier_semaphore()

    odd = lax.rem(c, 2)
    plane = c // 8
    lane = lax.rem(c, 8)
    across = 2 * s + plane

    def greet_row(i, _):
        pl.semaphore_signal(
            barrier,
            inc=1,
            device_id=(s, lax.rem(r + N // 2 + (i + 1) // 2 * (1 - 2 * lax.rem(i, 2)), N), c - odd + 1),
            device_id_type=MESH,
        )
        return 0

    def greet_col(i, _):
        pl.semaphore_signal(
            barrier, inc=1, device_id=(s, r, lax.rem(c + odd + 2 * i, N)), device_id_type=MESH
        )
        return 0

    def greet_side(i, _):
        pl.semaphore_signal(barrier, inc=1, device_id=(1 - s, r, 2 * i + 1), device_id_type=MESH)
        return 0


    @pl.when(odd == 1)
    def _():
        greet_col(0, 0)

    lax.fori_loop(1, N // 2, greet_col, 0)

    @pl.when(odd == 0)
    def _():
        pl.semaphore_signal(barrier, inc=1, device_id=(s, r, c + 1), device_id_type=MESH)

    lax.fori_loop(0, N - 1, greet_row, 0)
    lax.fori_loop(0, N // 2, greet_side, 0)

    loads = [
        pltpu.make_async_copy(src, dst, load_sem.at[i])
        for i, (src, dst) in enumerate(
            [
                (q_hbm, q_v),
                (k_hbm.at[s], k_v),
                (v_hbm.at[s], v_v),
                (nk_hbm, nk_v),
                (nv_hbm, nv_v),
                (res_hbm, res_v),
                (gain_hbm, gain_v),
                (ow_hbm, ow_v),
                (gw_hbm, gw_v),
                (uw_hbm, uw_v),
                (dw_hbm, dw_v),
                (len_hbm, len_ref),
            ]
        )
    ]
    for copy in loads:
        copy.start()

    def met_columns():
        @pl.when(odd == 0)
        def _():
            pl.semaphore_wait(barrier, N - 1)
            pl.semaphore_signal(met_sem, inc=1, device_id=(s, r, c + 1), device_id_type=MESH)

        @pl.when(odd == 1)
        def _():
            pl.semaphore_wait(met_sem, 1)

    def met_rows():
        @pl.when(odd == 1)
        def _():
            pl.semaphore_wait(barrier, 3 * N - 1)
            pl.semaphore_signal(met_sem, inc=1, device_id=(s, r, c - 1), device_id_type=MESH)

        @pl.when(odd == 0)
        def _():
            pl.semaphore_wait(met_sem, 1)

    def rows_at(ref, at, rows):
        return ref.at[pl.ds(pl.multiple_of(at * rows, rows), rows)]

    def offset(p):
        half = (p + 1) // 2
        return N + half * (2 * lax.rem(p, 2) - 1)

    def send(phase, source, target, device):
        pltpu.make_async_remote_copy(
            src_ref=source,
            dst_ref=target,
            send_sem=send_sem.at[phase],
            recv_sem=recv_sem.at[phase],
            device_id=device,
            device_id_type=MESH,
        ).start()

    def each(first, last, step):
        def one(i, _):
            step(i)
            return 0

        lax.fori_loop(first, last, one, 0)

    def to_columns(phase, source, target):
        def one(i):
            half = (i + 1) // 2
            peer = lax.rem(c + N // 2 + half * (1 - 2 * lax.rem(i, 2)), N)
            send(phase, source(peer), target, (s, r, peer))

        each(0, N - 1, one)

    def arrived(phase, ref):
        pltpu.make_async_copy(ref, ref, recv_sem.at[phase]).wait()

    def sent(phase, ref):
        pltpu.make_async_copy(ref, ref, send_sem.at[phase]).wait()

    qbd[...] = jnp.zeros_like(qbd)
    loads[0].wait()
    query = q_v[...].astype(F32)
    for t in range(2):
        mine = jnp.where(s == 0, query[t, 0:1, :], query[t, 1:2, :])
        for h in range(KV * 8):
            g = h // 8
            one_head = mine[:, h * HD : (h + 1) * HD]
            qbd[2 * h + t : 2 * h + t + 1, g * HD : (g + 1) * HD] = one_head
            heads[h // 2, 2 * (h % 2) + t : 2 * (h % 2) + t + 1, :] = one_head
    loads[1].wait()
    loads[11].wait()
    scale = 1.0 / math.sqrt(HD)
    scores = (
        lax.dot_general(
            qbd[...].astype(BF16), k_v[...], (((1,), (1,)), ((), ())), preferred_element_type=F32
        )
        * scale
    )
    live = c * SPAN + lax.broadcasted_iota(jnp.int32, scores.shape, 1) < len_ref[s]
    scores = jnp.where(live, scores, VERY_LOW)
    peak = jnp.max(scores, axis=1, keepdims=True).astype(BF16).astype(F32)
    weights = jnp.where(live, jnp.exp(scores - peak), 0.0)
    total = jnp.sum(weights, axis=1, keepdims=True)
    loads[2].wait()
    summed = jnp.dot(weights.astype(BF16), v_v[...], preferred_element_type=F32)
    low_lane = lax.broadcasted_iota(jnp.int32, (64, HD), 1) < HD // 2
    stats = jnp.where(low_lane, peak, total)
    for o in range(N):
        g = o // 4
        st_a32[8 * o : 8 * o + 4, :] = summed[4 * o : 4 * o + 4, g * HD : (g + 1) * HD]
        st_a32[8 * o + 4 : 8 * o + 8, :] = stats[4 * o : 4 * o + 4, :]

    st_a[...] = st_a32[...].reshape(N, 8, HD).astype(BF16)
    met_columns()
    to_columns(0, lambda peer: st_a.at[peer], rc_a.at[c])
    rc_a[c] = st_a[c]

    group_lanes = pl.ds(pl.multiple_of((c // 4) * HD, HD), HD)
    for copy in loads[3:8]:
        copy.wait()
    q4 = heads[c]
    fresh_k = nk_v[:, :, group_lanes].astype(F32)
    fresh_v = nv_v[:, :, group_lanes].astype(F32)
    nk = [jnp.where(s == 0, fresh_k[t, 0:1, :], fresh_k[t, 1:2, :]) for t in range(2)]
    nv = [jnp.where(s == 0, fresh_v[t, 0:1, :], fresh_v[t, 1:2, :]) for t in range(2)]
    second = lax.rem(lax.broadcasted_iota(jnp.int32, (4, HD), 0), 2) == 1
    f0 = jnp.broadcast_to(jnp.sum(q4 * nk[0], axis=1, keepdims=True) * scale, (4, HD))
    f1 = jnp.broadcast_to(jnp.sum(q4 * nk[1], axis=1, keepdims=True) * scale, (4, HD))
    f1 = jnp.where(second, f1, VERY_LOW)
    at = lax.broadcasted_iota(jnp.int32, (2 * N, 4 * N), 0)
    other = lax.rem(r + offset(at // 8 * 4 + lax.rem(at, 4)), N)
    wanted = lax.rem(at // 4, 2) * 2 * N + 2 * other + s
    chosen = lax.broadcasted_iota(jnp.int32, (2 * N, 4 * N), 1) == wanted
    res_s[...] = jnp.dot(
        jnp.where(chosen, 1.0, 0.0).astype(BF16), res_v[...].reshape(4 * N, 512), preferred_element_type=F32
    )
    gains = gain_v[...].astype(F32).reshape(1, 512)

    arrived(0, rc_a.at[pl.ds(0, N - 1)])
    blocks = rc_a[...].astype(F32)
    sums, stat = blocks[:, 0:4, :], blocks[:, 4:8, :]
    low = lax.broadcasted_iota(jnp.int32, (N, 4, HD), 2) < HD // 2
    turned = pltpu.roll(stat, HD // 2, 2)
    peaks = jnp.where(low, stat, turned)
    totals = jnp.where(low, turned, stat)
    top = jnp.maximum(jnp.max(peaks, axis=0), jnp.maximum(f0, f1))
    share = jnp.exp(peaks - top[None])
    e0 = jnp.exp(f0 - top)
    e1 = jnp.where(second, jnp.exp(f1 - top), 0.0)
    whole = jnp.sum(share * totals, axis=0) + e0 + e1
    mixed = jnp.sum(share * sums, axis=0) + e0 * nv[0] + e1 * nv[1]
    st_b[...] = (mixed / whole).astype(BF16).astype(F32)

    met_rows()
    def give_attended(k):
        def one(i):
            p = 4 * k + 3 - i
            send(1 + k, st_b, rc_b.at[p], (s, lax.rem(r + 2 * N - offset(p), N), c))

        each(0, 4 if k else 3, one)

    for k in range(3, -1, -1):
        give_attended(k)
    rc_b[0] = st_b[...]

    def project(k):
        attended = jnp.concatenate(
            [
                jnp.concatenate([rc_b[4 * k : 4 * k + 4, 2 * j + t, :] for j in range(2)], axis=1)
                for t in range(2)
            ],
            axis=0,
        )
        st_c[k] = jnp.dot(attended.astype(BF16), ow_v[...], preferred_element_type=F32).astype(BF16)
        to_columns(5 + k, lambda peer: st_c.at[k], rc_c.at[k, c])
        rc_c[k, c] = st_c[k]

    def scatter(ref, value, count, stride, base):
        for t in range(2):
            for m in range(count):
                ref[pl.ds(base + 2 * m + t, 4, stride=stride), :] = value[
                    4 * t : 4 * (t + 1), m * HD : (m + 1) * HD
                ]

    def lift(k):
        mid = res_s[8 * k : 8 * (k + 1), :] + jnp.sum(rc_c[k].astype(F32), axis=0)
        lifted = (mid * gains).astype(BF16)
        squares = jnp.broadcast_to(jnp.sum(mid * mid, axis=1, keepdims=True), (8, HD))
        high = squares.astype(BF16).astype(F32)
        base = 128 * k
        scatter(st_e32, high, 1, 32, base + 14)
        scatter(st_e32, squares - high, 1, 32, base + 30)
        if k == 0:
            loads[8].wait()
        scatter(st_e32, jnp.dot(lifted, gw_v[...], preferred_element_type=F32), 7, 32, base)
        if k == 0:
            loads[9].wait()
        scatter(st_e32, jnp.dot(lifted, uw_v[...], preferred_element_type=F32), 7, 32, base + 16)
        st_e[base : base + 128, :] = st_e32[base : base + 128, :].astype(BF16)

        def one(p):
            owner = lax.rem(r + N // 2 + offset(p), N)
            send(9, rows_at(st_e, p, 32), rows_at(rc_e, p, 32), (s, owner, c))

        each(4 * k, 4 * k + (4 if k < 3 else 3), one)
        at = 4 * s + 3 - k
        for t in range(2):
            for i in range(4):
                mid_t[at, 4 * t + 3 - i : 4 * t + 4 - i, :] = mid[4 * t + i : 4 * t + i + 1, :]

    arrived(1, rc_b.at[pl.ds(0, 3)])
    project(0)
    arrived(2, rc_b.at[pl.ds(0, 4)])
    project(1)
    arrived(3, rc_b.at[pl.ds(0, 4)])
    project(2)
    arrived(4, rc_b.at[pl.ds(0, 4)])
    project(3)
    arrived(5, rc_c.at[0, pl.ds(0, N - 1)])
    lift(0)
    arrived(6, rc_c.at[1, pl.ds(0, N - 1)])
    lift(1)
    arrived(7, rc_c.at[2, pl.ds(0, N - 1)])
    lift(2)
    arrived(8, rc_c.at[3, pl.ds(0, N - 1)])
    lift(3)
    rc_e[32 * (N - 1) :, :] = st_e[32 * (N - 1) :, :]
    arrived(9, rc_e.at[pl.ds(0, 32 * (N - 1))])
    lifts = jnp.sum(rc_e[...].astype(F32).reshape(N, 32, HD), axis=0)
    gate, up = lifts[0:16], lifts[16:32]
    inv0 = lax.rsqrt((gate[14:15] + up[14:15]) / D + 1e-05)
    inv1 = lax.rsqrt((gate[15:16] + up[15:16]) / D + 1e-05)
    inv = jnp.where(lax.rem(lax.broadcasted_iota(jnp.int32, (16, HD), 0), 2) == 1, inv1, inv0)
    gate, up = gate * inv, up * inv
    st_f[...] = (gate / (1.0 + jnp.exp(-gate)) * up).astype(BF16)

    def give_act(k):
        def one(i):
            p = 4 * k + 3 - i
            send(10 + k, st_f, rows_at(rc_f, p, 16), (s, lax.rem(r + 2 * N - offset(p), N), c))

        each(0, 4 if k else 3, one)

    for k in range(3, -1, -1):
        give_act(k)
    rc_f[0:16, :] = st_f[...]
    for k in range(4):
        send(22, mid_t.at[4 * s + k], mid_t.at[4 * s + k], (1 - s, r, c))
    target = lax.broadcasted_iota(jnp.int32, (4 * N, 4 * N), 0)
    source = lax.broadcasted_iota(jnp.int32, (4 * N, 4 * N), 1)
    row = lax.rem(r + N // 2 + offset(source // 16 * 4 + lax.rem(source, 4)), N)
    lands = lax.rem(source // 4, 2) * 2 * N + 2 * row + lax.rem(source // 8, 2)
    order[...] = jnp.where(target == lands, 1.0, 0.0).astype(BF16)
    loads[10].wait()

    def down(k):
        f32f[64 * k : 64 * (k + 1), :] = rc_f[64 * k : 64 * (k + 1), :].astype(F32)
        act = jnp.concatenate(
            [
                jnp.concatenate(
                    [f32f[pl.ds(64 * k + 2 * m + t, 4, stride=16), :] for m in range(7)], axis=1
                )
                for t in range(2)
            ],
            axis=0,
        )
        part = jnp.dot(act.astype(BF16), dw_v[...], preferred_element_type=F32)
        st_g[k] = part.astype(BF16)

        def one(i):
            send(14 + k, st_g.at[k], rc_g.at[k, lane], (s, r, 8 * plane + lax.rem(lane + i, 8)))

        each(1, 8, one)
        rc_g[k, lane] = st_g[k]

    def hand_on(k):
        st_x[k] = jnp.sum(rc_g[k].astype(F32), axis=0).astype(BF16)
        for i in (2, 1, 3):
            other = lax.rem(across + i, 4)
            send(18 + k, st_x.at[k], rc_x.at[k, across], (other // 2, r, 8 * lax.rem(other, 2) + lane))
        rc_x[k, across] = st_x[k]

    def finish(k):
        for side in range(2):
            parts = rc_x[k, 2 * side].astype(F32) + rc_x[k, 2 * side + 1].astype(F32)
            both[k, side] = (mid_t[4 * side + k] + parts).astype(BF16)

    arrived(10, rc_f.at[pl.ds(0, 48)])
    down(0)
    arrived(11, rc_f.at[pl.ds(0, 64)])
    down(1)
    arrived(12, rc_f.at[pl.ds(0, 64)])
    down(2)
    arrived(13, rc_f.at[pl.ds(0, 64)])
    down(3)
    arrived(14, rc_g.at[0, pl.ds(0, 7)])
    hand_on(0)
    arrived(15, rc_g.at[1, pl.ds(0, 7)])
    hand_on(1)
    arrived(16, rc_g.at[2, pl.ds(0, 7)])
    hand_on(2)
    arrived(17, rc_g.at[3, pl.ds(0, 7)])
    hand_on(3)
    arrived(22, mid_t.at[pl.ds(0, 4)])
    arrived(18, rc_x.at[0, pl.ds(0, 3)])
    finish(0)
    arrived(19, rc_x.at[1, pl.ds(0, 3)])
    finish(1)
    arrived(20, rc_x.at[2, pl.ds(0, 3)])
    finish(2)
    arrived(21, rc_x.at[3, pl.ds(0, 3)])
    finish(3)
    rows = both[...].astype(F32).reshape(4 * N, 512).astype(BF16)
    result = jnp.dot(order[...], rows, preferred_element_type=F32)
    out_ref[...] = result.astype(BF16).reshape(2, 2 * N, 512)

    sent(0, rc_a.at[pl.ds(0, N - 1)])
    sent(1, rc_b.at[pl.ds(0, 3)])
    sent(2, rc_b.at[pl.ds(0, 4)])
    sent(3, rc_b.at[pl.ds(0, 4)])
    sent(4, rc_b.at[pl.ds(0, 4)])
    sent(5, rc_c.at[0, pl.ds(0, N - 1)])
    sent(6, rc_c.at[1, pl.ds(0, N - 1)])
    sent(7, rc_c.at[2, pl.ds(0, N - 1)])
    sent(8, rc_c.at[3, pl.ds(0, N - 1)])
    sent(9, rc_e.at[pl.ds(0, 32 * (N - 1))])
    sent(10, rc_f.at[pl.ds(0, 48)])
    sent(11, rc_f.at[pl.ds(0, 64)])
    sent(12, rc_f.at[pl.ds(0, 64)])
    sent(13, rc_f.at[pl.ds(0, 64)])
    sent(14, rc_g.at[0, pl.ds(0, 7)])
    sent(15, rc_g.at[1, pl.ds(0, 7)])
    sent(16, rc_g.at[2, pl.ds(0, 7)])
    sent(17, rc_g.at[3, pl.ds(0, 7)])
    sent(18, rc_x.at[0, pl.ds(0, 3)])
    sent(19, rc_x.at[1, pl.ds(0, 3)])
    sent(20, rc_x.at[2, pl.ds(0, 3)])
    sent(21, rc_x.at[3, pl.ds(0, 3)])
    sent(22, mid_t.at[pl.ds(0, 4)])


def shards(query, new_keys, new_values, key_cache, value_cache, lengths, residual, out_weight,
           norm_gain, gate_weight, up_weight, down_weight):
    def vm(*shape, kind=F32):
        return pltpu.VMEM(shape, kind)

    hbm = pl.BlockSpec(memory_space=pltpu.HBM)
    return pl.pallas_call(
        kernel,
        out_shape=jax.ShapeDtypeStruct((2, 2 * N, 512), BF16),
        in_specs=[hbm] * 12,
        out_specs=pl.BlockSpec(memory_space=pltpu.VMEM),
        scratch_shapes=[
            pltpu.SMEM((2,), jnp.int32),
            vm(2, 2, 4096, kind=BF16),
            vm(2, 2, 512, kind=BF16),
            vm(2, 2, 512, kind=BF16),
            vm(SPAN, 512, kind=BF16),
            vm(SPAN, 512, kind=BF16),
            vm(2, 32, 512, kind=BF16),
            vm(256, 512, kind=BF16),
            vm(512, kind=BF16),
            vm(512, 896, kind=BF16),
            vm(512, 896, kind=BF16),
            vm(896, 512, kind=BF16),
            vm(64, 512),
            vm(N, 4, HD),
            vm(2 * N, 512),
            vm(8, 8, 512),
            vm(8 * N, HD), vm(N, 8, HD, kind=BF16), vm(N, 8, HD, kind=BF16),
            vm(4, HD), vm(N, 4, HD),
            vm(4, 8, 512, kind=BF16), vm(4, N, 8, 512, kind=BF16),
            vm(32 * N, HD), vm(32 * N, HD, kind=BF16), vm(32 * N, HD, kind=BF16),
            vm(16, HD, kind=BF16), vm(16 * N, HD, kind=BF16), vm(16 * N, HD),
            vm(4, 8, 512, kind=BF16), vm(4, 8, 8, 512, kind=BF16),
            vm(4, 8, 512, kind=BF16), vm(4, 4, 8, 512, kind=BF16),
            vm(4, 2, 8, 512, kind=BF16),
            vm(4 * N, 4 * N, kind=BF16),
            pltpu.SemaphoreType.DMA((12,)),
            pltpu.SemaphoreType.DMA((23,)),
            pltpu.SemaphoreType.DMA((23,)),
            pltpu.SemaphoreType.REGULAR,
        ],
        compiler_params=pltpu.CompilerParams(
            collective_id=0, has_side_effects=True, vmem_limit_bytes=32 * 1024 * 1024
        ),
        name="layer",
    )(*[
        pltpu.with_memory_space_constraint(a, pltpu.HBM)
        for a in (lengths, query, new_keys, new_values, key_cache, value_cache, residual, out_weight,
                  norm_gain, gate_weight, up_weight, down_weight)
    ])


def solution(mesh):
    in_specs = (
        P(None, "row", None),
        P(None, "row", None),
        P(None, "row", None),
        P("row", "col", None),
        P("row", "col", None),
        P("row"),
        P(None, None, "row"),
        P("col", "row"),
        P("row"),
        P("row", "col"),
        P("row", "col"),
        P("col", "row"),
    )
    out_specs = P(None, None, "row")
    return jax.shard_map(shards, mesh=mesh, in_specs=in_specs, out_specs=out_specs, check_vma=False)
```
